32 devices in a mesh: dp: 16 (over z, x, core), expert: 2 (over y).
Axes of the slice: x: 2, y: 2, z: 4, core: 2. Of those that a mesh axis runs over, the one named last changes fastest.
Arguments:
- tokens: bfloat16 [4096, 3584], P(('dp', 'expert')), may hold values from -6 to 6
- cotangent: bfloat16 [4096, 3584], P(('dp', 'expert')), may hold values from -6 to 6
- experts: int32 [4096, 2], P(('dp', 'expert')), may hold values from 0 to 63, all different within a row
- route_weight: float32 [4096, 2], P(('dp', 'expert')), may hold values from 0.05 to 1
- w_gate: bfloat16 [2, 7168, 3584], P('expert', 'dp'), may hold values from -0.09375 to 0.09375
- w_up: bfloat16 [2, 7168, 3584], P('expert', 'dp'), may hold values from -0.09375 to 0.09375
- w_down: bfloat16 [2, 7168, 3584], P('expert', 'dp'), may hold values from -0.0625 to 0.0625
Outputs:
- token_grad: bfloat16 [4096, 3584], P(('dp', 'expert'))
- grad_gate: bfloat16 [2, 7168, 3584], P('expert', 'dp')
- grad_up: bfloat16 [2, 7168, 3584], P('expert', 'dp')
- grad_down: bfloat16 [2, 7168, 3584], P('expert', 'dp')
The draws below stay inside these ranges and needn't reach their ends.
Inputs may be any that keep to these rules, and one draw needn't show every extreme that they name: Each token names 2 different experts of the 64.
All inputs are finite; a program needn't handle non-finite values.
Results may differ from the reference program's by a relative error of at most 0.024.
Values may be sent and summed in bfloat16 or wider, within the bound.
A program may use at most 128 MiB of HBM per device.

```python
import jax
import jax.numpy as jnp
from jax import lax

D = 3584
FF = 7168
ALL_EXPERTS = 64
TOP = 2
TOK_DEV = 128
CAP = 4
WINDOW = 2
TOKENS = 4096
N_DP = 16


def levels(own_key, shape, split, low, top_value):
    def one(dim, blocks):
        steps = jax.random.uniform(jax.random.fold_in(jax.random.fold_in(own_key, 6), dim), (blocks,), jnp.float32, low / len(split), top_value / len(split))
        return jnp.repeat(jnp.exp(steps), shape[dim] // blocks).reshape((-1,) + (1,) * (len(shape) - dim - 1))

    level = one(*split[0])
    for cut in split[1:]:
        level = level * one(*cut)
    return level


def picks_of(stream_key, rows, amount, top, lift):
    sequence = jax.random.permutation(jax.random.fold_in(stream_key, 1), amount)
    boost = sequence
    for power in range(3):
        boost = boost * boost // amount
    boost = boost * lift // amount
    chance = jax.random.randint(jax.random.fold_in(stream_key, 2), (rows, amount), 0, 4096) + boost
    fixed_rows = jax.random.permutation(jax.random.fold_in(stream_key, 3), rows)[jnp.arange(amount) % rows]
    chance = jnp.where(jnp.arange(rows)[:, None] == fixed_rows[None, :], 1 << 14, chance)
    priority = chance * amount + jnp.arange(amount)
    return lax.top_k(priority.astype(jnp.int32), top)[1].astype(jnp.int32)


def gaussian(rng, extent, spread, limit, shards=(), kind=jnp.bfloat16):
    entries = jax.random.normal(rng, extent, jnp.float32) * spread
    if len(shards) > 0:
        entries = levels(rng, extent, shards, -0.22, 0.18) * entries
    return jnp.clip(entries, min=-limit, max=limit).astype(kind)


def setup_inputs(seed: int = 0) -> dict:
    arg_keys = jax.random.split(jax.random.key(seed), 8)
    tokens = gaussian(arg_keys[0], (TOKENS, D), 1.0, 6.0, ((0, 32),))
    cotangent = gaussian(arg_keys[1], (TOKENS, D), 1.0, 6.0, ((0, 32),))
    experts = picks_of(arg_keys[2], TOKENS, ALL_EXPERTS, TOP, 256)
    route_weight = jnp.clip(0.05 + 0.95 * jax.random.uniform(arg_keys[3], (TOKENS, TOP), jnp.float32) ** levels(arg_keys[3], (TOKENS, TOP), ((0, 32),), -0.2, 0.2), 0.05, 1.0)
    w_gate = gaussian(arg_keys[4], (WINDOW, FF, D), D ** -0.5, 0.09375, ((0, 2), (1, 16)))
    w_up = gaussian(arg_keys[5], (WINDOW, FF, D), D ** -0.5, 0.09375, ((0, 2), (1, 16)))
    w_down = gaussian(arg_keys[6], (WINDOW, FF, D), FF ** -0.5, 0.0625, ((0, 2), (1, 16)))
    return dict(tokens=tokens, cotangent=cotangent, experts=experts, route_weight=route_weight, w_gate=w_gate, w_up=w_up, w_down=w_down)


def slot_table(experts_local, window, capacity):
    flat = experts_local.reshape(-1).astype(jnp.int32)
    count = flat.shape[0]
    labels = jnp.arange(window, dtype=jnp.int32)
    onehot = (flat[:, None] == labels[None, :]).astype(jnp.int32)
    before = jnp.cumsum(onehot, axis=0) - onehot
    slot = jnp.sum(before * onehot, axis=1).astype(jnp.int32)
    keep = (jnp.sum(onehot, axis=1) > 0) & (slot < capacity)
    target = jnp.where(keep, flat * capacity + slot, -1)
    places = jnp.arange(window * capacity, dtype=jnp.int32)
    match = (target[None, :] == places[:, None]).astype(jnp.int32)
    source = jnp.sum(match * jnp.arange(count, dtype=jnp.int32)[None, :], axis=1).astype(jnp.int32)
    filled = jnp.sum(match, axis=1) > 0
    return flat, slot, keep, source, filled


def fill_slots(tokens_local, cot_local, weight_flat, source, filled, top):
    which = source // top
    x_slots = jnp.where(filled[:, None], tokens_local[which], jnp.zeros((), tokens_local.dtype))
    scaled = weight_flat[source][:, None] * cot_local[which].astype(jnp.float32)
    c_slots = jnp.where(filled[:, None], scaled, jnp.float32(0.0)).astype(jnp.bfloat16)
    return x_slots, c_slots


def gather_back(slot_grad_local, flat, slot, keep, capacity, top):
    index = jnp.where(keep, flat * capacity + slot, 0).astype(jnp.int32)
    picked = jnp.where(keep[:, None], slot_grad_local[index].astype(jnp.float32), jnp.float32(0.0))
    return picked.reshape(-1, top, picked.shape[-1]).sum(axis=1).astype(jnp.bfloat16)


def reference(tokens, cotangent, experts, route_weight, w_gate, w_up, w_down):
    blocks = TOKENS // TOK_DEV
    tok_blocks = tokens.reshape(blocks, TOK_DEV, D)
    cot_blocks = cotangent.reshape(blocks, TOK_DEV, D)
    exp_blocks = experts.reshape(blocks, TOK_DEV, TOP)
    wt_blocks = route_weight.reshape(blocks, TOK_DEV * TOP)
    flat, slot, keep, source, filled = jax.vmap(lambda e: slot_table(e, WINDOW, CAP))(exp_blocks)
    x_slots, c_slots = jax.vmap(lambda t, c, w, s, f: fill_slots(t, c, w, s, f, TOP))(tok_blocks, cot_blocks, wt_blocks, source, filled)
    x_all = x_slots.reshape(blocks, WINDOW, CAP, D)
    c_all = c_slots.reshape(blocks, WINDOW, CAP, D)
    group = FF // N_DP
    grads_gate = []
    grads_up = []
    grads_down = []
    slot_parts = []
    for expert in range(WINDOW):
        x_rows = x_all[:, expert].reshape(-1, D)
        c_rows = c_all[:, expert].reshape(-1, D)
        gate = jnp.dot(x_rows, w_gate[expert].T, preferred_element_type=jnp.float32)
        up = jnp.dot(x_rows, w_up[expert].T, preferred_element_type=jnp.float32)
        sig = jax.nn.sigmoid(gate)
        act = gate * sig
        hidden = (act * up).astype(jnp.bfloat16)
        back = jnp.dot(c_rows, w_down[expert].T, preferred_element_type=jnp.float32)
        d_gate = (back * up * sig * (1.0 + gate * (1.0 - sig))).astype(jnp.bfloat16)
        d_up = (back * act).astype(jnp.bfloat16)
        grads_gate.append(jnp.dot(d_gate.T, x_rows, preferred_element_type=jnp.float32).astype(jnp.bfloat16))
        grads_up.append(jnp.dot(d_up.T, x_rows, preferred_element_type=jnp.float32).astype(jnp.bfloat16))
        grads_down.append(jnp.dot(hidden.T, c_rows, preferred_element_type=jnp.float32).astype(jnp.bfloat16))
        total = jnp.zeros((x_rows.shape[0], D), jnp.float32)
        for index in range(N_DP):
            lo = index * group
            hi = lo + group
            part = jnp.dot(d_gate[:, lo:hi], w_gate[expert][lo:hi], preferred_element_type=jnp.float32) + jnp.dot(d_up[:, lo:hi], w_up[expert][lo:hi], preferred_element_type=jnp.float32)
            total = total + part.astype(jnp.bfloat16).astype(jnp.float32)
        slot_parts.append(total.astype(jnp.bfloat16).reshape(blocks, CAP, D))
    slot_grad = jnp.stack(slot_parts, axis=1).reshape(blocks, WINDOW * CAP, D)
    token_grad = jax.vmap(lambda g, f, s, k: gather_back(g, f, s, k, CAP, TOP))(slot_grad, flat, slot, keep)
    return (token_grad.reshape(TOKENS, D), jnp.stack(grads_gate), jnp.stack(grads_up), jnp.stack(grads_down))
```

```python
import functools

import jax
import jax.numpy as jnp
import numpy as np
from jax import lax
from jax.experimental import pallas as pl
from jax.experimental.pallas import tpu as pltpu
from jax.sharding import PartitionSpec as P

CAP = 4
MESH = pl.DeviceIdType.MESH
F32 = jnp.float32
BF16 = jnp.bfloat16
NT = (((1,), (1,)), ((), ()))


def one_hots(experts, place_expert, place_slot):
    count = experts.shape[0]
    first = experts[:, 0:1] == place_expert
    second = experts[:, 1:2] == place_expert
    named = jnp.where(first | second, 1.0, 0.0).astype(F32)
    shape = (count, count)
    earlier = lax.broadcasted_iota(jnp.int32, shape, 1) < lax.broadcasted_iota(jnp.int32, shape, 0)
    earlier = jnp.where(earlier, 1.0, 0.0).astype(BF16)
    before = jnp.dot(earlier, named.astype(BF16), preferred_element_type=F32)
    return jnp.where(before == place_slot.astype(F32), named, 0.0), first


def exchange_kernel(
    n_dp, window,
    tokens, cotangent, experts, weights, select, w_gate, w_up, w_down,
    rows_out, d_out, back_out, pick_out,
    w, sent, arrived, rows, prod, d_rows, part, sib, out_buf, in_buf,
    w_sem, y_send, y_recv, ring_send, ring_recv, sib_send, sib_recv,
    pair_send, pair_recv, rs_send, rs_recv, z_send, z_recv, local_sem,
):
    width = tokens.shape[1]
    half = width // 2
    quarter = half // 2
    hidden = w_gate.shape[0]
    chips = n_dp // 2
    far = chips // 2
    group = 2 * CAP
    kept = window * CAP
    block = window * group
    total = n_dp * block

    me = lax.axis_index("dp")
    mine = lax.axis_index("expert")
    core = lax.rem(me, 2)
    chip = lax.div(me, 2)
    spot = jnp.where(lax.rem(chip, 2) == 0, lax.div(chip, 2), chips - 1 - lax.div(chip, 2))

    def chip_at(place):
        place = lax.rem(place + 2 * chips, chips)
        return jnp.where(place < far, 2 * place, 2 * (chips - 1 - place) + 1)

    def at(place):
        return 2 * chip_at(place) + core

    sibling = (2 * chip + 1 - core, mine)
    neighbour = ((at(spot + 1), mine), (at(spot - 1), mine))

    loads = []
    for index, source in enumerate((w_gate, w_up, w_down)):
        loads.append(pltpu.make_async_copy(source, w.at[pl.ds(index * hidden, hidden), :], w_sem.at[index]))
        loads[-1].start()

    barrier = pltpu.get_barrier_semaphore()
    greet = [sibling, *neighbour]
    for step in range(1, window):
        greet.append((me, lax.rem(mine + step, window)))
    for device in greet:
        pl.semaphore_signal(barrier, inc=1, device_id=device, device_id_type=MESH)

    lanes = max(128, block)
    place = lax.broadcasted_iota(jnp.int32, (1, lanes), 1)
    match, first = one_hots(experts[...], lax.div(place, group), lax.rem(place, CAP))
    match_t = jnp.transpose(match)[:block]
    scale = jnp.transpose(jnp.where(first, weights[:, 0:1], weights[:, 1:2]) * match)[:block]
    scale = jnp.sum(scale, axis=1, keepdims=True)
    is_x = lax.rem(lax.broadcasted_iota(jnp.int32, match_t.shape, 0), group) < CAP
    slots = jnp.dot(jnp.where(is_x, match_t, 0.0).astype(BF16), tokens[...], preferred_element_type=F32)
    slots += scale * jnp.dot(
        jnp.where(is_x, 0.0, match_t).astype(BF16), cotangent[...], preferred_element_type=F32
    )
    for e in range(window):
        piece = slots[e * group:(e + 1) * group]
        sent[e] = jnp.concatenate([piece[:, :half], piece[:, half:]], axis=0).astype(BF16)

    pl.semaphore_wait(barrier, len(greet))

    swaps = []
    for step in range(1, window):
        other = lax.rem(mine + step, window)
        swaps.append(pltpu.make_async_remote_copy(
            src_ref=sent.at[other], dst_ref=arrived.at[mine],
            send_sem=y_send.at[step], recv_sem=y_recv.at[step],
            device_id=(me, other), device_id_type=MESH,
        ))
        swaps[-1].start()
    arrived[mine] = sent[mine]

    columns = window * 2 * kept
    place = lax.broadcasted_iota(jnp.int32, (1, columns), 1)
    row = lax.rem(place, kept)
    match, _ = one_hots(experts[...], lax.div(place, 2 * kept), lax.rem(row, CAP))
    match = jnp.where(lax.div(row, CAP) == mine, match, 0.0)
    side = lax.rem(lax.div(place, kept), 2)
    for h in range(2):
        pick_out[h] = jnp.where(side == h, match, 0.0).astype(BF16)

    for copy in swaps:
        copy.wait_recv()
    for h in range(2):
        own = [arrived[s].astype(F32)[h * group:(h + 1) * group] for s in range(window)]
        rows[me, :, pl.ds(h * half, half)] = jnp.concatenate(own, axis=0).astype(BF16)

    def hop(way, step, h):
        origin = at(spot - step) if way == 0 else at(spot + step)
        view = rows.at[origin, :, pl.ds(h * half, half)]
        return pltpu.make_async_remote_copy(
            src_ref=view, dst_ref=view,
            send_sem=ring_send.at[way, step, h], recv_sem=ring_recv.at[way, step, h],
            device_id=neighbour[way], device_id_type=MESH,
        )

    def share(way, step, h):
        origin = at(spot - step) if way == 0 else at(spot + step)
        view = rows.at[origin, :, pl.ds(h * half, half)]
        return pltpu.make_async_remote_copy(
            src_ref=view, dst_ref=view,
            send_sem=sib_send.at[way, step, h], recv_sem=sib_recv.at[way, step, h],
            device_id=sibling, device_id_type=MESH,
        )

    def travels(way, step, h):
        return step < far - 1 or (step == far - 1 and way == h)

    hops, shares = [], []
    for h in range(2):
        for way in range(2):
            hops.append(hop(way, 0, h))
            hops[-1].start()
    for h in range(2):
        shares.append(share(0, 0, h))
        shares[-1].start()
    for step in range(far):
        for h in range(2):
            for way in range(2):
                if travels(way, step, h):
                    hop(way, step, h).wait_recv()
                    if travels(way, step + 1, h):
                        hops.append(hop(way, step + 1, h))
                        hops[-1].start()
                    shares.append(share(way, step + 1, h))
                    shares[-1].start()
    for copy in loads:
        copy.wait()
    for copy in shares:
        copy.wait_recv()
    gathered = pltpu.make_async_copy(rows, rows_out, local_sem)
    gathered.start()

    wide = 256 if total % 256 == 0 else total
    deep = 512
    blocks = wide // block
    tall = 32

    def products(n, carry):
        start = pl.multiple_of(n * wide, wide)

        def chunk(k, carry):
            at_k = pl.ds(pl.multiple_of(k * deep, deep), deep)
            piece = rows[pl.ds(n * blocks, blocks), :, at_k].reshape(wide, deep)
            term = lax.dot_general(w[:, at_k], piece, NT, preferred_element_type=F32)

            @pl.when(k == 0)
            def _():
                prod[...] = term

            @pl.when(k > 0)
            def _():
                prod[...] += term

            return carry

        lax.fori_loop(0, width // deep, chunk, 0)

        def pointwise(i, carry):
            def rows_of(index):
                return pl.ds(pl.multiple_of(index * hidden + i * tall, tall), tall)

            gate = prod[rows_of(0), :]
            up = prod[rows_of(1), :]
            back = pltpu.roll(prod[rows_of(2), :], wide - CAP, 1)
            sig = jax.nn.sigmoid(gate)
            act = gate * sig
            lane = lax.broadcasted_iota(jnp.int32, gate.shape, 1)
            is_x = lax.rem(lane, group) < CAP
            hid = pltpu.roll(act * up, CAP, 1)
            d_gate = back * up * sig * (1.0 + gate * (1.0 - sig))
            d_up = back * act
            cols = pl.ds(start, wide)
            d_out[rows_of(0), cols] = jnp.where(is_x, d_gate, 0.0).astype(BF16)
            d_out[rows_of(1), cols] = jnp.where(is_x, d_up, 0.0).astype(BF16)
            d_out[rows_of(2), cols] = jnp.where(is_x, 0.0, hid).astype(BF16)
            return carry

        lax.fori_loop(0, hidden // tall, pointwise, 0)
        return carry

    lax.fori_loop(0, total // wide, products, 0)

    d_rows[...] = lax.dot_general(
        select[...], d_out[pl.ds(0, 2 * hidden), :], NT, preferred_element_type=F32
    ).astype(BF16)
    narrow = 256

    def terms(i, carry):
        sides = []
        for h in range(2):
            cols = pl.ds(pl.multiple_of(h * half + i * narrow, narrow), narrow)
            term = jnp.dot(d_rows[...], w[pl.ds(0, 2 * hidden), cols], preferred_element_type=F32)
            sides.append(term.reshape(n_dp, kept, narrow))
        both = jnp.concatenate(sides, axis=1).astype(BF16)
        part[:, :, pl.ds(pl.multiple_of(i * narrow, narrow), narrow)] = both
        return carry

    lax.fori_loop(0, half // narrow, terms, 0)

    def pair(k_offset):
        k = chip_at(spot + k_offset)
        return pltpu.make_async_remote_copy(
            src_ref=part.at[(1 - core) * chips + k], dst_ref=sib.at[k],
            send_sem=pair_send.at[k_offset], recv_sem=pair_recv.at[k_offset],
            device_id=sibling, device_id_type=MESH,
        )

    offsets = [far]
    for step in range(far - 1, 0, -1):
        offsets += [step, chips - step]
    offsets.append(0)
    pairs = {}
    for offset in offsets:
        pairs[offset] = pair(offset)
        pairs[offset].start()

    def rs(way, step, h):
        cols = pl.ds(h * quarter, quarter)
        return pltpu.make_async_remote_copy(
            src_ref=out_buf.at[way, step, :, cols], dst_ref=in_buf.at[way, step, :, cols],
            send_sem=rs_send.at[way, step, h], recv_sem=rs_recv.at[way, step, h],
            device_id=neighbour[way], device_id_type=MESH,
        )

    def begins(way, step, h):
        return step > 0 or way == h

    ready = set()
    sums = []
    for step in range(far):
        distance = far - step
        for h in range(2):
            cols = pl.ds(h * quarter, quarter)
            for way in range(2):
                if not begins(way, step, h):
                    continue
                offset = distance if way == 0 else chips - distance
                if offset not in ready:
                    pairs[offset].wait_recv()
                    ready.add(offset)
                k = chip_at(spot + offset)
                value = part[core * chips + k, :, cols].astype(F32) + sib[k, :, cols].astype(F32)
                if step > 0 and begins(way, step - 1, h):
                    rs(way, step - 1, h).wait_recv()
                    value += in_buf[way, step - 1, :, cols].astype(F32)
                out_buf[way, step, :, cols] = value.astype(BF16)
                rs(way, step, h).start()
                sums.append((way, step, h))
    pairs[0].wait_recv()
    own = part[core * chips + chip].astype(F32) + sib[chip].astype(F32)
    for way in range(2):
        for h in range(2):
            rs(way, far - 1, h).wait_recv()
        own += in_buf[way, far - 1].astype(F32)
    back_out[mine] = own.astype(BF16)

    returns = []
    for step in range(1, window):
        other = lax.rem(mine + step, window)
        returns.append(pltpu.make_async_remote_copy(
            src_ref=back_out.at[mine], dst_ref=back_out.at[mine],
            send_sem=z_send.at[step], recv_sem=z_recv.at[step],
            device_id=(me, other), device_id_type=MESH,
        ))
        returns[-1].start()
    for copy in swaps + hops + shares:
        copy.wait_send()
    for copy in pairs.values():
        copy.wait_send()
    for key in sums:
        rs(*key).wait_send()
    for copy in returns:
        copy.wait()
    gathered.wait()


def gradient_kernel(hidden, rows, d, back, pick, token_grad, grad_gate, grad_up, grad_down):
    for index, out in enumerate((grad_gate, grad_up, grad_down)):
        out[...] = jnp.dot(
            d[pl.ds(index * hidden, hidden), :], rows[...], preferred_element_type=F32
        ).astype(out.dtype)
    token_grad[...] = jnp.dot(pick[0], back[...], preferred_element_type=F32).astype(token_grad.dtype)


def selection(n_dp, window):
    chips, kept, group = n_dp // 2, window * CAP, 2 * CAP
    table = np.zeros((n_dp * kept, n_dp * window * group), np.float32)
    for core in range(2):
        for chip in range(chips):
            for row in range(kept):
                source, slot = divmod(row, CAP)
                column = (2 * chip + core) * window * group + source * group + slot
                table[(core * chips + chip) * kept + row, column] = 1.0
    return table


def shards(n_dp, window, tokens, cotangent, experts, route_weight, w_gate, w_up, w_down):
    count, width = tokens.shape
    hidden = w_gate.shape[1]
    half = width // 2
    chips = n_dp // 2
    far = chips // 2
    kept = window * CAP
    block = 2 * kept
    total = n_dp * block
    wide = 256 if total % 256 == 0 else total
    vmem = pl.BlockSpec(memory_space=pltpu.VMEM)
    anywhere = pl.BlockSpec(memory_space=pl.ANY)
    dma = pltpu.SemaphoreType.DMA
    flops = 2 * hidden * width * total
    rows, d, back, pick = pl.pallas_call(
        functools.partial(exchange_kernel, n_dp, window),
        out_shape=(
            jax.ShapeDtypeStruct((n_dp, block, width), BF16),
            jax.ShapeDtypeStruct((3 * hidden, total), BF16),
            jax.ShapeDtypeStruct((window, block, half), BF16),
            jax.ShapeDtypeStruct((2, count, window * block), BF16),
        ),
        in_specs=[vmem] * 5 + [anywhere] * 3,
        out_specs=(anywhere, vmem, vmem, vmem),
        scratch_shapes=[
            pltpu.VMEM((3 * hidden, width), BF16),
            pltpu.VMEM((window, 4 * CAP, half), BF16),
            pltpu.VMEM((window, 4 * CAP, half), BF16),
            pltpu.VMEM((n_dp, block, width), BF16),
            pltpu.VMEM((3 * hidden, wide), F32),
            pltpu.VMEM((n_dp * kept, 2 * hidden), BF16),
            pltpu.VMEM((n_dp, block, half), BF16),
            pltpu.VMEM((chips, block, half), BF16),
            pltpu.VMEM((2, far, block, half), BF16),
            pltpu.VMEM((2, far, block, half), BF16),
            dma((3,)),
            dma((window,)),
            dma((window,)),
            dma((2, far, 2)),
            dma((2, far, 2)),
            dma((2, far + 1, 2)),
            dma((2, far + 1, 2)),
            dma((chips,)),
            dma((chips,)),
            dma((2, far, 2)),
            dma((2, far, 2)),
            dma((window,)),
            dma((window,)),
            dma,
        ],
        compiler_params=pltpu.CompilerParams(
            collective_id=0, has_side_effects=True, vmem_limit_bytes=60 * 1024 * 1024
        ),
        cost_estimate=pl.CostEstimate(
            flops=5 * flops, bytes_accessed=2 * (3 * hidden + 2 * count + total) * width, transcendentals=0
        ),
        name="exchange",
    )(
        tokens, cotangent, experts, route_weight, jnp.asarray(selection(n_dp, window), BF16),
        w_gate[0], w_up[0], w_down[0],
    )

    step = half // 2
    grads = jax.ShapeDtypeStruct((hidden, width), BF16)
    token_grad, grad_g, grad_u, grad_d = pl.pallas_call(
        functools.partial(gradient_kernel, hidden),
        grid=(4,),
        out_shape=(jax.ShapeDtypeStruct((count, width), BF16), grads, grads, grads),
        in_specs=[
            pl.BlockSpec((total, step), lambda i: (0, i)),
            pl.BlockSpec((3 * hidden, total), lambda i: (0, 0)),
            pl.BlockSpec((window * block, step), lambda i: (0, lax.rem(i, 2))),
            pl.BlockSpec((1, count, window * block), lambda i: (lax.div(i, 2), 0, 0)),
        ],
        out_specs=(
            pl.BlockSpec((count, step), lambda i: (0, i)),
            *[pl.BlockSpec((hidden, step), lambda i: (0, i))] * 3,
        ),
        compiler_params=pltpu.CompilerParams(vmem_limit_bytes=60 * 1024 * 1024),
        cost_estimate=pl.CostEstimate(
            flops=3 * flops, bytes_accessed=2 * (3 * hidden + count + total) * width, transcendentals=0
        ),
        name="gradients",
    )(rows.reshape(total, width), d, back.reshape(window * block, half), pick)
    return token_grad, grad_g[None], grad_u[None], grad_d[None]


def solution(mesh):
    by_token = P(("dp", "expert"), None)
    by_expert = P("expert", "dp", None)
    return jax.shard_map(
        functools.partial(shards, mesh.shape["dp"], mesh.shape["expert"]),
        mesh=mesh,
        in_specs=(by_token,) * 4 + (by_expert,) * 3,
        out_specs=(by_token,) + (by_expert,) * 3,
        check_vma=False,
    )
```

```python
import functools

import jax
import jax.numpy as jnp
from jax import lax
from jax.experimental import pallas as pl
from jax.experimental.pallas import tpu as pltpu
from jax.sharding import PartitionSpec as P

CAP = 4
MESH = pl.DeviceIdType.MESH
F32 = jnp.float32
BF16 = jnp.bfloat16
NT = (((1,), (1,)), ((), ()))


def one_hots(experts, place_expert, place_slot):
    count = experts.shape[1]
    first = experts[0:1, :] == place_expert
    second = experts[1:2, :] == place_expert
    named = jnp.where(first | second, 1.0, 0.0).astype(F32)
    shape = (count, count)
    earlier = lax.broadcasted_iota(jnp.int32, shape, 0) < lax.broadcasted_iota(jnp.int32, shape, 1)
    earlier = jnp.where(earlier, 1.0, 0.0).astype(BF16)
    before = jnp.dot(named.astype(BF16), earlier, preferred_element_type=F32)
    return jnp.where(before == place_slot.astype(F32), named, 0.0), first


def exchange_kernel(
    n_dp, window,
    tokens, cotangent, experts, weights, w_gate, w_up, w_down,
    rows_out, d_out, back_out, pick_out,
    w, sent, arrived, rows, prod, d_rows, part, sib, out_buf, in_buf,
    w_sem, y_send, y_recv, ring_send, ring_recv, sib_send, sib_recv,
    pair_send, pair_recv, rs_send, rs_recv, z_send, z_recv, local_sem,
):
    width = tokens.shape[1]
    half = width // 2
    quarter = half // 2
    hidden = w_gate.shape[0]
    chips = n_dp // 2
    far = chips // 2
    group = 2 * CAP
    kept = window * CAP
    block = window * group
    total = n_dp * block

    me = lax.axis_index("dp")
    mine = lax.axis_index("expert")
    core = lax.rem(me, 2)
    chip = lax.div(me, 2)
    spot = jnp.where(lax.rem(chip, 2) == 0, lax.div(chip, 2), chips - 1 - lax.div(chip, 2))

    def chip_at(place):
        place = lax.rem(place + 2 * chips, chips)
        return jnp.where(place < far, 2 * place, 2 * (chips - 1 - place) + 1)

    def at(place):
        return 2 * chip_at(place) + core

    sibling = (2 * chip + 1 - core, mine)
    neighbour = ((at(spot + 1), mine), (at(spot - 1), mine))

    loads = []
    for index, source in enumerate((w_gate, w_up, w_down)):
        loads.append(pltpu.make_async_copy(source, w.at[pl.ds(index * hidden, hidden), :], w_sem.at[index]))
        loads[-1].start()

    barrier = pltpu.get_barrier_semaphore()
    greet = [sibling, *neighbour]
    for step in range(1, window):
        greet.append((me, lax.rem(mine + step, window)))
    for device in greet:
        pl.semaphore_signal(barrier, inc=1, device_id=device, device_id_type=MESH)

    place = lax.broadcasted_iota(jnp.int32, (block, 1), 0)
    match, first = one_hots(experts[...], lax.div(place, group), lax.rem(place, CAP))
    scale = jnp.where(first, weights[0:1, :], weights[1:2, :]) * match
    scale = jnp.sum(scale, axis=1, keepdims=True)
    is_x = lax.rem(lax.broadcasted_iota(jnp.int32, match.shape, 0), group) < CAP
    slots = jnp.dot(jnp.where(is_x, match, 0.0).astype(BF16), tokens[...], preferred_element_type=F32)
    slots += scale * jnp.dot(
        jnp.where(is_x, 0.0, match).astype(BF16), cotangent[...], preferred_element_type=F32
    )
    for e in range(window):
        piece = slots[e * group:(e + 1) * group]
        sent[e] = jnp.concatenate([piece[:, :half], piece[:, half:]], axis=0).astype(BF16)

    pl.semaphore_wait(barrier, len(greet))

    swaps = []
    for step in range(1, window):
        other = lax.rem(mine + step, window)
        swaps.append(pltpu.make_async_remote_copy(
            src_ref=sent.at[other], dst_ref=arrived.at[mine],
            send_sem=y_send.at[step], recv_sem=y_recv.at[step],
            device_id=(me, other), device_id_type=MESH,
        ))
        swaps[-1].start()
    arrived[mine] = sent[mine]

    columns = window * 2 * kept
    place = lax.broadcasted_iota(jnp.int32, (columns, 1), 0)
    row = lax.rem(place, kept)
    match, _ = one_hots(experts[...], lax.div(place, 2 * kept), lax.rem(row, CAP))
    match = jnp.transpose(jnp.where(lax.div(row, CAP) == mine, match, 0.0))
    side = lax.rem(lax.div(lax.broadcasted_iota(jnp.int32, (1, columns), 1), kept), 2)
    for h in range(2):
        pick_out[h] = jnp.where(side == h, match, 0.0).astype(BF16)

    for copy in swaps:
        copy.wait_recv()
    for h in range(2):
        own = [arrived[s].astype(F32)[h * group:(h + 1) * group] for s in range(window)]
        rows[me, :, pl.ds(h * half, half)] = jnp.concatenate(own, axis=0).astype(BF16)

    def view(way, step, q):
        origin = at(spot - step) if way == 0 else at(spot + step)
        return rows.at[origin, :, pl.ds(q * quarter, quarter)]

    def hop(way, step, q):
        return pltpu.make_async_remote_copy(
            src_ref=view(way, step, q), dst_ref=view(way, step, q),
            send_sem=ring_send.at[way, step, q], recv_sem=ring_recv.at[way, step, q],
            device_id=neighbour[way], device_id_type=MESH,
        )

    def share(way, step, q):
        return pltpu.make_async_remote_copy(
            src_ref=view(way, step, q), dst_ref=view(way, step, q),
            send_sem=sib_send.at[way, step, q], recv_sem=sib_recv.at[way, step, q],
            device_id=sibling, device_id_type=MESH,
        )

    def travels(way, step, q):
        return step < far - 1 or (step == far - 1 and way == q % 2)

    hops, shares = [], [[], []]
    for q in range(4):
        for way in range(2):
            if travels(way, 0, q):
                hops.append(hop(way, 0, q))
                hops[-1].start()
    for q in range(4):
        shares[q // 2].append(share(0, 0, q))
        shares[q // 2][-1].start()
    for step in range(far):
        for q in range(4):
            for way in range(2):
                if travels(way, step, q):
                    hop(way, step, q).wait_recv()
                    if travels(way, step + 1, q):
                        hops.append(hop(way, step + 1, q))
                        hops[-1].start()
                    shares[q // 2].append(share(way, step + 1, q))
                    shares[q // 2][-1].start()
    for copy in loads:
        copy.wait()

    wide = 256 if total % 256 == 0 else total
    blocks = wide // block
    tall = 32
    x_lane = lax.rem(lax.broadcasted_iota(jnp.int32, (tall, wide), 1), group) < CAP

    def multiply(n, h):
        def matrix(index, carry):
            at_f = pl.ds(pl.multiple_of(index * hidden, hidden), hidden)
            at_k = pl.ds(h * half, half)
            piece = rows[pl.ds(n * blocks, blocks), :, at_k].reshape(wide, half)
            term = lax.dot_general(w[at_f, at_k], piece, NT, preferred_element_type=F32)
            prod[n, at_f, :] = term if h == 0 else prod[n, at_f, :] + term
            return carry

        lax.fori_loop(0, 3, matrix, 0)

    def first_half(n, carry):
        multiply(n, 0)
        return carry

    def products(n, carry):
        multiply(n, 1)
        start = pl.multiple_of(n * wide, wide)

        def pointwise(i, carry):
            def rows_of(index):
                return pl.ds(pl.multiple_of(index * hidden + i * tall, tall), tall)

            gate = prod[n, rows_of(0), :]
            up = prod[n, rows_of(1), :]
            back = pltpu.roll(prod[n, rows_of(2), :], wide - CAP, 1)
            sig = jax.nn.sigmoid(gate)
            act = gate * sig
            hid = pltpu.roll(act * up, CAP, 1)
            d_gate = back * up * sig * (1.0 + gate * (1.0 - sig))
            d_up = back * act
            cols = pl.ds(start, wide)
            d_out[rows_of(0), cols] = jnp.where(x_lane, d_gate, 0.0).astype(BF16)
            d_out[rows_of(1), cols] = jnp.where(x_lane, d_up, 0.0).astype(BF16)
            d_out[rows_of(2), cols] = jnp.where(x_lane, 0.0, hid).astype(BF16)
            return carry

        lax.fori_loop(0, hidden // tall, pointwise, 0)
        return carry

    for copy in shares[0]:
        copy.wait_recv()
    lax.fori_loop(0, total // wide, first_half, 0)
    for copy in shares[1]:
        copy.wait_recv()
    gathered = pltpu.make_async_copy(rows, rows_out, local_sem)
    gathered.start()
    lax.fori_loop(0, total // wide, products, 0)

    ordinal = lax.broadcasted_iota(jnp.int32, (n_dp * kept, 1), 0)
    owner = 2 * lax.rem(lax.div(ordinal, kept), chips) + lax.div(ordinal, kept * chips)
    slot = lax.rem(ordinal, kept)
    source = owner * block + lax.div(slot, CAP) * group + lax.rem(slot, CAP)
    select = lax.broadcasted_iota(jnp.int32, (n_dp * kept, total), 1) == source
    d_rows[...] = lax.dot_general(
        jnp.where(select, 1.0, 0.0).astype(BF16), d_out[pl.ds(0, 2 * hidden), :], NT, preferred_element_type=F32
    ).astype(BF16)
    narrow = 256
    chunks = half // narrow
    edges = (0, (chunks + 1) // 2 * narrow, half)

    def lanes_of(h):
        return pl.ds(edges[h], edges[h + 1] - edges[h])

    def terms(i, carry):
        sides = []
        for side in range(2):
            cols = pl.ds(pl.multiple_of(side * half + i * narrow, narrow), narrow)
            term = jnp.dot(d_rows[...], w[pl.ds(0, 2 * hidden), cols], preferred_element_type=F32)
            sides.append(term.reshape(n_dp, kept, narrow))
        both = jnp.concatenate(sides, axis=1).astype(BF16)
        part[:, :, pl.ds(pl.multiple_of(i * narrow, narrow), narrow)] = both
        return carry

    def pair(offset, h):
        k = chip_at(spot + offset)
        return pltpu.make_async_remote_copy(
            src_ref=part.at[(1 - core) * chips + k, :, lanes_of(h)], dst_ref=sib.at[k, :, lanes_of(h)],
            send_sem=pair_send.at[offset, h], recv_sem=pair_recv.at[offset, h],
            device_id=sibling, device_id_type=MESH,
        )

    offsets = [far]
    for step in range(far - 1, 0, -1):
        offsets += [step, chips - step]
    offsets.append(0)
    pairs = {}
    for h in range(2):
        lax.fori_loop(edges[h] // narrow, edges[h + 1] // narrow, terms, 0)
        for offset in offsets:
            pairs[offset, h] = pair(offset, h)
            pairs[offset, h].start()

    def rs(way, step, h):
        return pltpu.make_async_remote_copy(
            src_ref=out_buf.at[way, step, :, lanes_of(h)], dst_ref=in_buf.at[way, step, :, lanes_of(h)],
            send_sem=rs_send.at[way, step, h], recv_sem=rs_recv.at[way, step, h],
            device_id=neighbour[way], device_id_type=MESH,
        )

    def begins(way, step, h):
        return step > 0 or way == h

    ready = set()
    sums = []
    for step in range(far):
        distance = far - step
        for h in range(2):
            cols = lanes_of(h)
            for way in range(2):
                if not begins(way, step, h):
                    continue
                offset = distance if way == 0 else chips - distance
                if (offset, h) not in ready:
                    pairs[offset, h].wait_recv()
                    ready.add((offset, h))
                k = chip_at(spot + offset)
                value = part[core * chips + k, :, cols].astype(F32) + sib[k, :, cols].astype(F32)
                if step > 0 and begins(way, step - 1, h):
                    rs(way, step - 1, h).wait_recv()
                    value += in_buf[way, step - 1, :, cols].astype(F32)
                out_buf[way, step, :, cols] = value.astype(BF16)
                rs(way, step, h).start()
                sums.append((way, step, h))
    for h in range(2):
        pairs[0, h].wait_recv()
    own = part[core * chips + chip].astype(F32) + sib[chip].astype(F32)
    for way in range(2):
        for h in range(2):
            rs(way, far - 1, h).wait_recv()
        own += in_buf[way, far - 1].astype(F32)
    back_out[mine] = own.astype(BF16)

    returns = []
    for step in range(1, window):
        other = lax.rem(mine + step, window)
        returns.append(pltpu.make_async_remote_copy(
            src_ref=back_out.at[mine], dst_ref=back_out.at[mine],
            send_sem=z_send.at[step], recv_sem=z_recv.at[step],
            device_id=(me, other), device_id_type=MESH,
        ))
        returns[-1].start()
    for copy in swaps + hops + shares[0] + shares[1]:
        copy.wait_send()
    for copy in pairs.values():
        copy.wait_send()
    for key in sums:
        rs(*key).wait_send()
    for copy in returns:
        copy.wait()
    gathered.wait()


def gradient_kernel(hidden, rows, d, back, pick, token_grad, grad_gate, grad_up, grad_down):
    for index, out in enumerate((grad_gate, grad_up, grad_down)):
        out[...] = jnp.dot(
            d[pl.ds(index * hidden, hidden), :], rows[...], preferred_element_type=F32
        ).astype(out.dtype)
    token_grad[...] = jnp.dot(pick[0], back[...], preferred_element_type=F32).astype(token_grad.dtype)


def shards(n_dp, window, tokens, cotangent, experts, route_weight, w_gate, w_up, w_down):
    count, width = tokens.shape
    hidden = w_gate.shape[1]
    half = width // 2
    chips = n_dp // 2
    far = chips // 2
    kept = window * CAP
    block = 2 * kept
    total = n_dp * block
    wide = 256 if total % 256 == 0 else total
    vmem = pl.BlockSpec(memory_space=pltpu.VMEM)
    anywhere = pl.BlockSpec(memory_space=pl.ANY)
    dma = pltpu.SemaphoreType.DMA
    flops = 2 * hidden * width * total
    rows, d, back, pick = pl.pallas_call(
        functools.partial(exchange_kernel, n_dp, window),
        out_shape=(
            jax.ShapeDtypeStruct((n_dp, block, width), BF16),
            jax.ShapeDtypeStruct((3 * hidden, total), BF16),
            jax.ShapeDtypeStruct((window, block, half), BF16),
            jax.ShapeDtypeStruct((2, count, window * block), BF16),
        ),
        in_specs=[vmem] * 4 + [anywhere] * 3,
        out_specs=(anywhere, vmem, vmem, vmem),
        scratch_shapes=[
            pltpu.VMEM((3 * hidden, width), BF16),
            pltpu.VMEM((window, 4 * CAP, half), BF16),
            pltpu.VMEM((window, 4 * CAP, half), BF16),
            pltpu.VMEM((n_dp, block, width), BF16),
            pltpu.VMEM((total // wide, 3 * hidden, wide), F32),
            pltpu.VMEM((n_dp * kept, 2 * hidden), BF16),
            pltpu.VMEM((n_dp, block, half), BF16),
            pltpu.VMEM((chips, block, half), BF16),
            pltpu.VMEM((2, far, block, half), BF16),
            pltpu.VMEM((2, far, block, half), BF16),
            dma((3,)),
            dma((window,)),
            dma((window,)),
            dma((2, far, 4)),
            dma((2, far, 4)),
            dma((2, far + 1, 4)),
            dma((2, far + 1, 4)),
            dma((chips, 2)),
            dma((chips, 2)),
            dma((2, far, 2)),
            dma((2, far, 2)),
            dma((window,)),
            dma((window,)),
            dma,
        ],
        compiler_params=pltpu.CompilerParams(
            collective_id=0, has_side_effects=True, vmem_limit_bytes=60 * 1024 * 1024
        ),
        cost_estimate=pl.CostEstimate(
            flops=5 * flops, bytes_accessed=2 * (3 * hidden + 2 * count + total) * width, transcendentals=0
        ),
        name="exchange",
    )(
        tokens, cotangent, experts.T, route_weight.T,
        w_gate[0], w_up[0], w_down[0],
    )

    step = half // 2
    grads = jax.ShapeDtypeStruct((hidden, width), BF16)
    token_grad, grad_g, grad_u, grad_d = pl.pallas_call(
        functools.partial(gradient_kernel, hidden),
        grid=(4,),
        out_shape=(jax.ShapeDtypeStruct((count, width), BF16), grads, grads, grads),
        in_specs=[
            pl.BlockSpec((total, step), lambda i: (0, i)),
            pl.BlockSpec((3 * hidden, total), lambda i: (0, 0)),
            pl.BlockSpec((window * block, step), lambda i: (0, lax.rem(i, 2))),
            pl.BlockSpec((1, count, window * block), lambda i: (lax.div(i, 2), 0, 0)),
        ],
        out_specs=(
            pl.BlockSpec((count, step), lambda i: (0, i)),
            *[pl.BlockSpec((hidden, step), lambda i: (0, i))] * 3,
        ),
        compiler_params=pltpu.CompilerParams(vmem_limit_bytes=60 * 1024 * 1024),
        cost_estimate=pl.CostEstimate(
            flops=3 * flops, bytes_accessed=2 * (3 * hidden + count + total) * width, transcendentals=0
        ),
        name="gradients",
    )(rows.reshape(total, width), d, back.reshape(window * block, half), pick)
    return token_grad, grad_g[None], grad_u[None], grad_d[None]


def solution(mesh):
    by_token = P(("dp", "expert"), None)
    by_expert = P("expert", "dp", None)
    return jax.shard_map(
        functools.partial(shards, mesh.shape["dp"], mesh.shape["expert"]),
        mesh=mesh,
        in_specs=(by_token,) * 4 + (by_expert,) * 3,
        out_specs=(by_token,) + (by_expert,) * 3,
        check_vma=False,
    )
```

```python
import functools

import jax
import jax.numpy as jnp
from jax import lax
from jax.experimental import pallas as pl
from jax.experimental.pallas import tpu as pltpu
from jax.sharding import PartitionSpec as P

CAP = 4
MESH = pl.DeviceIdType.MESH
F32 = jnp.float32
BF16 = jnp.bfloat16
NT = (((1,), (1,)), ((), ()))


def one_hots(experts, place_expert, place_slot):
    count = experts.shape[1]
    first = experts[0:1, :] == place_expert
    second = experts[1:2, :] == place_expert
    named = jnp.where(first | second, 1.0, 0.0).astype(F32)
    shape = (count, count)
    earlier = lax.broadcasted_iota(jnp.int32, shape, 0) < lax.broadcasted_iota(jnp.int32, shape, 1)
    earlier = jnp.where(earlier, 1.0, 0.0).astype(BF16)
    before = jnp.dot(named.astype(BF16), earlier, preferred_element_type=F32)
    return jnp.where(before == place_slot.astype(F32), named, 0.0), first


def exchange_kernel(
    n_dp, window,
    tokens, cotangent, experts, weights, w_gate, w_up, w_down,
    grads_out, back_out, pick_out,
    returned, d_out, w, sent, arrived, rows, prod, d_rows, part, sib, out_buf, in_buf,
    w_sem, y_send, y_recv, ring_send, ring_recv, sib_send, sib_recv,
    pair_send, pair_recv, rs_send, rs_recv, z_send, z_recv,
):
    width = tokens.shape[1]
    half = width // 2
    quarter = half // 2
    hidden = w_gate.shape[0]
    chips = n_dp // 2
    far = chips // 2
    group = 2 * CAP
    kept = window * CAP
    block = window * group
    total = n_dp * block

    me = lax.axis_index("dp")
    mine = lax.axis_index("expert")
    core = lax.rem(me, 2)
    chip = lax.div(me, 2)
    spot = jnp.where(lax.rem(chip, 2) == 0, lax.div(chip, 2), chips - 1 - lax.div(chip, 2))

    def chip_at(place):
        place = lax.rem(place + 2 * chips, chips)
        return jnp.where(place < far, 2 * place, 2 * (chips - 1 - place) + 1)

    def at(place):
        return 2 * chip_at(place) + core

    sibling = (2 * chip + 1 - core, mine)
    neighbour = ((at(spot + 1), mine), (at(spot - 1), mine))

    loads = []
    for index, source in enumerate((w_gate, w_up, w_down)):
        loads.append(pltpu.make_async_copy(source, w.at[pl.ds(index * hidden, hidden), :], w_sem.at[index]))
        loads[-1].start()

    barrier = pltpu.get_barrier_semaphore()
    greet = [sibling, *neighbour]
    for step in range(1, window):
        greet.append((me, lax.rem(mine + step, window)))
    for device in greet:
        pl.semaphore_signal(barrier, inc=1, device_id=device, device_id_type=MESH)

    place = lax.broadcasted_iota(jnp.int32, (block, 1), 0)
    match, first = one_hots(experts[...], lax.div(place, group), lax.rem(place, CAP))
    scale = jnp.where(first, weights[0:1, :], weights[1:2, :]) * match
    scale = jnp.sum(scale, axis=1, keepdims=True)
    is_x = lax.rem(lax.broadcasted_iota(jnp.int32, match.shape, 0), group) < CAP
    slots = jnp.dot(jnp.where(is_x, match, 0.0).astype(BF16), tokens[...], preferred_element_type=F32)
    slots += scale * jnp.dot(
        jnp.where(is_x, 0.0, match).astype(BF16), cotangent[...], preferred_element_type=F32
    )
    for e in range(window):
        piece = slots[e * group:(e + 1) * group]
        sent[e] = jnp.concatenate([piece[:, :half], piece[:, half:]], axis=0).astype(BF16)

    pl.semaphore_wait(barrier, len(greet))

    swaps = []
    for step in range(1, window):
        other = lax.rem(mine + step, window)
        swaps.append(pltpu.make_async_remote_copy(
            src_ref=sent.at[other], dst_ref=arrived.at[mine],
            send_sem=y_send.at[step], recv_sem=y_recv.at[step],
            device_id=(me, other), device_id_type=MESH,
        ))
        swaps[-1].start()
    arrived[mine] = sent[mine]

    columns = window * 2 * kept
    place = lax.broadcasted_iota(jnp.int32, (columns, 1), 0)
    row = lax.rem(place, kept)
    match, _ = one_hots(experts[...], lax.div(place, 2 * kept), lax.rem(row, CAP))
    match = jnp.transpose(jnp.where(lax.div(row, CAP) == mine, match, 0.0))
    side = lax.rem(lax.div(lax.broadcasted_iota(jnp.int32, (1, columns), 1), kept), 2)
    for h in range(2):
        pick_out[h] = jnp.where(side == h, match, 0.0).astype(BF16)

    for copy in swaps:
        copy.wait_recv()
    for h in range(2):
        own = [arrived[s].astype(F32)[h * group:(h + 1) * group] for s in range(window)]
        rows[me, :, pl.ds(h * half, half)] = jnp.concatenate(own, axis=0).astype(BF16)

    def view(way, step, q):
        origin = at(spot - step) if way == 0 else at(spot + step)
        return rows.at[origin, :, pl.ds(q * quarter, quarter)]

    def hop(way, step, q):
        return pltpu.make_async_remote_copy(
            src_ref=view(way, step, q), dst_ref=view(way, step, q),
            send_sem=ring_send.at[way, step, q], recv_sem=ring_recv.at[way, step, q],
            device_id=neighbour[way], device_id_type=MESH,
        )

    def share(way, step, q):
        return pltpu.make_async_remote_copy(
            src_ref=view(way, step, q), dst_ref=view(way, step, q),
            send_sem=sib_send.at[way, step, q], recv_sem=sib_recv.at[way, step, q],
            device_id=sibling, device_id_type=MESH,
        )

    def travels(way, step, q):
        return step < far - 1 or (step == far - 1 and way == q % 2)

    hops, shares = [], [[], []]
    for q in range(4):
        for way in range(2):
            if travels(way, 0, q):
                hops.append(hop(way, 0, q))
                hops[-1].start()
    for q in range(4):
        shares[q // 2].append(share(0, 0, q))
        shares[q // 2][-1].start()
    for step in range(far):
        for q in range(4):
            for way in range(2):
                if travels(way, step, q):
                    hop(way, step, q).wait_recv()
                    if travels(way, step + 1, q):
                        hops.append(hop(way, step + 1, q))
                        hops[-1].start()
                    shares[q // 2].append(share(way, step + 1, q))
                    shares[q // 2][-1].start()
    for copy in loads:
        copy.wait()

    wide = 256 if total % 256 == 0 else total
    blocks = wide // block
    tall = 32
    x_lane = lax.rem(lax.broadcasted_iota(jnp.int32, (tall, wide), 1), group) < CAP

    def multiply(n, h):
        def matrix(index, carry):
            at_f = pl.ds(pl.multiple_of(index * hidden, hidden), hidden)
            at_k = pl.ds(h * half, half)
            piece = rows[pl.ds(n * blocks, blocks), :, at_k].reshape(wide, half)
            term = lax.dot_general(w[at_f, at_k], piece, NT, preferred_element_type=F32)
            prod[n, at_f, :] = term if h == 0 else prod[n, at_f, :] + term
            return carry

        lax.fori_loop(0, 3, matrix, 0)

    def first_half(n, carry):
        multiply(n, 0)
        return carry

    def products(n, carry):
        multiply(n, 1)
        start = pl.multiple_of(n * wide, wide)

        def pointwise(i, carry):
            def rows_of(index):
                return pl.ds(pl.multiple_of(index * hidden + i * tall, tall), tall)

            gate = prod[n, rows_of(0), :]
            up = prod[n, rows_of(1), :]
            back = pltpu.roll(prod[n, rows_of(2), :], wide - CAP, 1)
            sig = jax.nn.sigmoid(gate)
            act = gate * sig
            hid = pltpu.roll(act * up, CAP, 1)
            d_gate = back * up * sig * (1.0 + gate * (1.0 - sig))
            d_up = back * act
            cols = pl.ds(start, wide)
            d_out[rows_of(0), cols] = jnp.where(x_lane, d_gate, 0.0).astype(BF16)
            d_out[rows_of(1), cols] = jnp.where(x_lane, d_up, 0.0).astype(BF16)
            d_out[rows_of(2), cols] = jnp.where(x_lane, 0.0, hid).astype(BF16)
            return carry

        lax.fori_loop(0, hidden // tall, pointwise, 0)
        return carry

    for copy in shares[0]:
        copy.wait_recv()
    lax.fori_loop(0, total // wide, first_half, 0)
    for copy in shares[1]:
        copy.wait_recv()
    lax.fori_loop(0, total // wide, products, 0)

    ordinal = lax.broadcasted_iota(jnp.int32, (n_dp * kept, 1), 0)
    owner = 2 * lax.rem(lax.div(ordinal, kept), chips) + lax.div(ordinal, kept * chips)
    slot = lax.rem(ordinal, kept)
    source = owner * block + lax.div(slot, CAP) * group + lax.rem(slot, CAP)
    select = lax.broadcasted_iota(jnp.int32, (n_dp * kept, total), 1) == source
    d_rows[...] = lax.dot_general(
        jnp.where(select, 1.0, 0.0).astype(BF16), d_out[pl.ds(0, 2 * hidden), :], NT, preferred_element_type=F32
    ).astype(BF16)
    narrow = 256
    chunks = half // narrow
    edges = (0, (chunks + 1) // 2 * narrow, half)

    def lanes_of(h):
        return pl.ds(edges[h], edges[h + 1] - edges[h])

    def terms(i, carry):
        sides = []
        for side in range(2):
            cols = pl.ds(pl.multiple_of(side * half + i * narrow, narrow), narrow)
            term = jnp.dot(d_rows[...], w[pl.ds(0, 2 * hidden), cols], preferred_element_type=F32)
            sides.append(term.reshape(n_dp, kept, narrow))
        both = jnp.concatenate(sides, axis=1).astype(BF16)
        part[:, :, pl.ds(pl.multiple_of(i * narrow, narrow), narrow)] = both
        return carry

    def pair(offset, h):
        k = chip_at(spot + offset)
        return pltpu.make_async_remote_copy(
            src_ref=part.at[(1 - core) * chips + k, :, lanes_of(h)], dst_ref=sib.at[k, :, lanes_of(h)],
            send_sem=pair_send.at[offset, h], recv_sem=pair_recv.at[offset, h],
            device_id=sibling, device_id_type=MESH,
        )

    offsets = [far]
    for step in range(far - 1, 0, -1):
        offsets += [step, chips - step]
    offsets.append(0)
    pairs = {}
    for h in range(2):
        lax.fori_loop(edges[h] // narrow, edges[h + 1] // narrow, terms, 0)
        for offset in offsets:
            pairs[offset, h] = pair(offset, h)
            pairs[offset, h].start()

    def rs(way, step, h):
        return pltpu.make_async_remote_copy(
            src_ref=out_buf.at[way, step, :, lanes_of(h)], dst_ref=in_buf.at[way, step, :, lanes_of(h)],
            send_sem=rs_send.at[way, step, h], recv_sem=rs_recv.at[way, step, h],
            device_id=neighbour[way], device_id_type=MESH,
        )

    def begins(way, step, h):
        return step > 0 or way == h

    strip = 512

    def gradients(first, last):
        def strip_of(i, carry):
            cols = pl.ds(pl.multiple_of(i * strip, strip), strip)
            piece = rows[:, :, cols].reshape(total, strip)

            def matrix(index, carry):
                at_f = pl.ds(pl.multiple_of(index * hidden, hidden), hidden)
                grads_out[at_f, cols] = jnp.dot(d_out[at_f, :], piece, preferred_element_type=F32).astype(BF16)
                return carry

            return lax.fori_loop(0, 3, matrix, carry)

        lax.fori_loop(first, last, strip_of, 0)

    strips = width // strip
    marks = [strips * 2 * step // (2 * far + 1) for step in range(far + 1)]

    ready = set()
    sums = []
    for step in range(far):
        distance = far - step
        for h in range(2):
            cols = lanes_of(h)
            for way in range(2):
                if not begins(way, step, h):
                    continue
                offset = distance if way == 0 else chips - distance
                if (offset, h) not in ready:
                    pairs[offset, h].wait_recv()
                    ready.add((offset, h))
                k = chip_at(spot + offset)
                value = part[core * chips + k, :, cols].astype(F32) + sib[k, :, cols].astype(F32)
                if step > 0 and begins(way, step - 1, h):
                    rs(way, step - 1, h).wait_recv()
                    value += in_buf[way, step - 1, :, cols].astype(F32)
                out_buf[way, step, :, cols] = value.astype(BF16)
                rs(way, step, h).start()
                sums.append((way, step, h))
        gradients(marks[step], marks[step + 1])
    for h in range(2):
        pairs[0, h].wait_recv()
    own = part[core * chips + chip].astype(F32) + sib[chip].astype(F32)
    for way in range(2):
        for h in range(2):
            rs(way, far - 1, h).wait_recv()
        own += in_buf[way, far - 1].astype(F32)
    returned[mine] = own.astype(BF16)

    returns = []
    for step in range(1, window):
        other = lax.rem(mine + step, window)
        returns.append(pltpu.make_async_remote_copy(
            src_ref=returned.at[mine], dst_ref=returned.at[mine],
            send_sem=z_send.at[step], recv_sem=z_recv.at[step],
            device_id=(me, other), device_id_type=MESH,
        ))
        returns[-1].start()
    gradients(marks[far], strips)
    for copy in swaps + hops + shares[0] + shares[1]:
        copy.wait_send()
    for copy in pairs.values():
        copy.wait_send()
    for key in sums:
        rs(*key).wait_send()
    for copy in returns:
        copy.wait()
    back_out[...] = returned[...]


def finish_kernel(hidden, grads, back, pick, token_grad, grad_gate, grad_up, grad_down, sem):
    copies = []
    for index, out in enumerate((grad_gate, grad_up, grad_down)):
        copies.append(pltpu.make_async_copy(grads.at[pl.ds(index * hidden, hidden), :], out, sem.at[index]))
        copies[-1].start()
    window, block, half = back.shape
    returned = back[...].reshape(window * block, half)
    for h in range(2):
        term = jnp.dot(pick[h], returned, preferred_element_type=F32)
        token_grad[:, pl.ds(h * half, half)] = term.astype(token_grad.dtype)
    for copy in copies:
        copy.wait()


def shards(n_dp, window, tokens, cotangent, experts, route_weight, w_gate, w_up, w_down):
    count, width = tokens.shape
    hidden = w_gate.shape[1]
    half = width // 2
    chips = n_dp // 2
    far = chips // 2
    kept = window * CAP
    block = 2 * kept
    total = n_dp * block
    wide = 256 if total % 256 == 0 else total
    vmem = pl.BlockSpec(memory_space=pltpu.VMEM)
    anywhere = pl.BlockSpec(memory_space=pl.ANY)
    dma = pltpu.SemaphoreType.DMA
    flops = 2 * hidden * width * total
    grads, back, pick = pl.pallas_call(
        functools.partial(exchange_kernel, n_dp, window),
        out_shape=(
            pltpu.VMEM((3 * hidden, width), BF16),
            pltpu.VMEM((window, block, half), BF16),
            pltpu.VMEM((2, count, window * block), BF16),
        ),
        in_specs=[vmem] * 4 + [anywhere] * 3,
        out_specs=(vmem, vmem, vmem),
        scratch_shapes=[
            pltpu.VMEM((window, block, half), BF16),
            pltpu.VMEM((3 * hidden, total), BF16),
            pltpu.VMEM((3 * hidden, width), BF16),
            pltpu.VMEM((window, 4 * CAP, half), BF16),
            pltpu.VMEM((window, 4 * CAP, half), BF16),
            pltpu.VMEM((n_dp, block, width), BF16),
            pltpu.VMEM((total // wide, 3 * hidden, wide), F32),
            pltpu.VMEM((n_dp * kept, 2 * hidden), BF16),
            pltpu.VMEM((n_dp, block, half), BF16),
            pltpu.VMEM((chips, block, half), BF16),
            pltpu.VMEM((2, far, block, half), BF16),
            pltpu.VMEM((2, far, block, half), BF16),
            dma((3,)),
            dma((window,)),
            dma((window,)),
            dma((2, far, 4)),
            dma((2, far, 4)),
            dma((2, far + 1, 4)),
            dma((2, far + 1, 4)),
            dma((chips, 2)),
            dma((chips, 2)),
            dma((2, far, 2)),
            dma((2, far, 2)),
            dma((window,)),
            dma((window,)),
        ],
        compiler_params=pltpu.CompilerParams(
            collective_id=0, has_side_effects=True, vmem_limit_bytes=61 * 1024 * 1024 - 6 * hidden * width
        ),
        cost_estimate=pl.CostEstimate(
            flops=5 * flops, bytes_accessed=2 * (3 * hidden + 2 * count + total) * width, transcendentals=0
        ),
        name="exchange",
    )(
        tokens, cotangent, experts.T, route_weight.T,
        w_gate[0], w_up[0], w_down[0],
    )

    like = jax.ShapeDtypeStruct((hidden, width), BF16)
    token_grad, grad_g, grad_u, grad_d = pl.pallas_call(
        functools.partial(finish_kernel, hidden),
        out_shape=(jax.ShapeDtypeStruct((count, width), BF16), like, like, like),
        in_specs=[vmem] * 3,
        out_specs=(vmem, anywhere, anywhere, anywhere),
        scratch_shapes=[dma((3,))],
        compiler_params=pltpu.CompilerParams(vmem_limit_bytes=16 * 1024 * 1024),
        cost_estimate=pl.CostEstimate(
            flops=4 * count * window * block * half, bytes_accessed=2 * (3 * hidden + count) * width,
            transcendentals=0,
        ),
        name="finish",
    )(*(pltpu.with_memory_space_constraint(array, pltpu.VMEM) for array in (grads, back, pick)))
    return token_grad, grad_g[None], grad_u[None], grad_d[None]


def solution(mesh):
    by_token = P(("dp", "expert"), None)
    by_expert = P("expert", "dp", None)
    return jax.shard_map(
        functools.partial(shards, mesh.shape["dp"], mesh.shape["expert"]),
        mesh=mesh,
        in_specs=(by_token,) * 4 + (by_expert,) * 3,
        out_specs=(by_token,) + (by_expert,) * 3,
        check_vma=False,
    )
```

```python
import functools

import jax
import jax.numpy as jnp
from jax import lax
from jax.experimental import pallas as pl
from jax.experimental.pallas import tpu as pltpu
from jax.sharding import PartitionSpec as P

CAP = 4
MESH = pl.DeviceIdType.MESH
F32 = jnp.float32
BF16 = jnp.bfloat16
NT = (((1,), (1,)), ((), ()))


def one_hots(experts, place_expert, place_slot):
    count = experts.shape[1]
    first = experts[0:1, :] == place_expert
    second = experts[1:2, :] == place_expert
    named = jnp.where(first | second, 1.0, 0.0).astype(F32)
    shape = (count, count)
    earlier = lax.broadcasted_iota(jnp.int32, shape, 0) < lax.broadcasted_iota(jnp.int32, shape, 1)
    earlier = jnp.where(earlier, 1.0, 0.0).astype(BF16)
    before = jnp.dot(named.astype(BF16), earlier, preferred_element_type=F32)
    return jnp.where(before == place_slot.astype(F32), named, 0.0), first


def exchange_kernel(
    n_dp, window,
    tokens_in, cotangent_in, experts, weights, w_gate, w_up, w_down,
    grads_out, back_out, pick_out,
    tokens, cotangent, returned, d_out, w, sent, arrived, rows, prod, d_rows, part, sib, out_buf, in_buf,
    in_sem, w_sem, y_send, y_recv, ring_send, ring_recv, sib_send, sib_recv,
    pair_send, pair_recv, rs_send, rs_recv, z_send, z_recv,
):
    width = tokens_in.shape[1]
    half = width // 2
    quarter = half // 2
    hidden = w_gate.shape[0]
    chips = n_dp // 2
    far = chips // 2
    group = 2 * CAP
    kept = window * CAP
    block = window * group
    total = n_dp * block

    me = lax.axis_index("dp")
    mine = lax.axis_index("expert")
    core = lax.rem(me, 2)
    chip = lax.div(me, 2)
    spot = jnp.where(lax.rem(chip, 2) == 0, lax.div(chip, 2), chips - 1 - lax.div(chip, 2))

    def chip_at(place):
        place = lax.rem(place + 2 * chips, chips)
        return jnp.where(place < far, 2 * place, 2 * (chips - 1 - place) + 1)

    def at(place):
        return 2 * chip_at(place) + core

    sibling = (2 * chip + 1 - core, mine)
    neighbour = ((at(spot + 1), mine), (at(spot - 1), mine))

    inputs = []
    for p in range(2):
        cols = pl.ds(p * half, half)
        inputs.append([
            pltpu.make_async_copy(tokens_in.at[:, cols], tokens.at[:, cols], in_sem.at[0, p]),
            pltpu.make_async_copy(cotangent_in.at[:, cols], cotangent.at[:, cols], in_sem.at[1, p]),
        ])
        for copy in inputs[-1]:
            copy.start()

    barrier = pltpu.get_barrier_semaphore()
    greet = [sibling, *neighbour]
    for step in range(1, window):
        greet.append((me, lax.rem(mine + step, window)))
    for device in greet:
        pl.semaphore_signal(barrier, inc=1, device_id=device, device_id_type=MESH)

    place = lax.broadcasted_iota(jnp.int32, (block, 1), 0)
    match, first = one_hots(experts[...], lax.div(place, group), lax.rem(place, CAP))
    scale = jnp.where(first, weights[0:1, :], weights[1:2, :]) * match
    scale = jnp.sum(scale, axis=1, keepdims=True)
    is_x = lax.rem(lax.broadcasted_iota(jnp.int32, match.shape, 0), group) < CAP
    x_match = jnp.where(is_x, match, 0.0).astype(BF16)
    c_match = jnp.where(is_x, 0.0, match).astype(BF16)

    def swap(step, p):
        other = lax.rem(mine + step, window)
        lanes = pl.ds(p * quarter, quarter)
        return pltpu.make_async_remote_copy(
            src_ref=sent.at[other, :, lanes], dst_ref=arrived.at[mine, :, lanes],
            send_sem=y_send.at[step, p], recv_sem=y_recv.at[step, p],
            device_id=(me, other), device_id_type=MESH,
        )

    swaps, loads = [], []
    for p in range(2):
        cols = pl.ds(p * half, half)
        for copy in inputs[p]:
            copy.wait()
        slots = jnp.dot(x_match, tokens[:, cols], preferred_element_type=F32)
        slots += scale * jnp.dot(c_match, cotangent[:, cols], preferred_element_type=F32)
        lanes = pl.ds(p * quarter, quarter)
        for e in range(window):
            piece = slots[e * group:(e + 1) * group]
            sent[e, :, lanes] = jnp.concatenate([piece[:, :quarter], piece[:, quarter:]], axis=0).astype(BF16)
        if p == 0:
            pl.semaphore_wait(barrier, len(greet))
        swaps.append([swap(step, p) for step in range(1, window)])
        for copy in swaps[p]:
            copy.start()
        arrived[mine, :, lanes] = sent[mine, :, lanes]
    for index, source in enumerate((w_gate, w_up, w_down)):
        loads.append(pltpu.make_async_copy(source, w.at[pl.ds(index * hidden, hidden), :], w_sem.at[index]))
        loads[-1].start()

    def view(way, step, q):
        origin = at(spot - step) if way == 0 else at(spot + step)
        return rows.at[origin, :, pl.ds(q * quarter, quarter)]

    def hop(way, step, q):
        return pltpu.make_async_remote_copy(
            src_ref=view(way, step, q), dst_ref=view(way, step, q),
            send_sem=ring_send.at[way, step, q], recv_sem=ring_recv.at[way, step, q],
            device_id=neighbour[way], device_id_type=MESH,
        )

    def share(way, step, q):
        return pltpu.make_async_remote_copy(
            src_ref=view(way, step, q), dst_ref=view(way, step, q),
            send_sem=sib_send.at[way, step, q], recv_sem=sib_recv.at[way, step, q],
            device_id=sibling, device_id_type=MESH,
        )

    def travels(way, step, q):
        return step < far - 1 or (step == far - 1 and way == q % 2)

    hops, shares = [], [[], []]
    for p in range(2):
        for copy in swaps[p]:
            copy.wait_recv()
        for q in (2 * p, 2 * p + 1):
            side = (q % 2) * group
            lanes = pl.ds(p * quarter, quarter)
            own = [arrived[s, :, lanes].astype(F32)[side:side + group] for s in range(window)]
            rows[me, :, pl.ds(q * quarter, quarter)] = jnp.concatenate(own, axis=0).astype(BF16)
            for way in range(2):
                if travels(way, 0, q):
                    hops.append(hop(way, 0, q))
                    hops[-1].start()
            shares[p].append(share(0, 0, q))
            shares[p][-1].start()

    columns = window * 2 * kept
    place = lax.broadcasted_iota(jnp.int32, (columns, 1), 0)
    row = lax.rem(place, kept)
    match, _ = one_hots(experts[...], lax.div(place, 2 * kept), lax.rem(row, CAP))
    match = jnp.transpose(jnp.where(lax.div(row, CAP) == mine, match, 0.0))
    side = lax.rem(lax.div(lax.broadcasted_iota(jnp.int32, (1, columns), 1), kept), 2)
    for h in range(2):
        pick_out[h] = jnp.where(side == h, match, 0.0).astype(BF16)

    for step in range(far):
        for q in range(4):
            for way in range(2):
                if travels(way, step, q):
                    hop(way, step, q).wait_recv()
                    if travels(way, step + 1, q):
                        hops.append(hop(way, step + 1, q))
                        hops[-1].start()
                    shares[q // 2].append(share(way, step + 1, q))
                    shares[q // 2][-1].start()
    for copy in loads:
        copy.wait()

    wide = 256 if total % 256 == 0 else total
    blocks = wide // block
    tall = 112 if hidden % 112 == 0 else 16
    x_lane = lax.rem(lax.broadcasted_iota(jnp.int32, (tall, wide), 1), group) < CAP

    def multiply(n, h):
        def matrix(index, carry):
            at_f = pl.ds(pl.multiple_of(index * hidden, hidden), hidden)
            at_k = pl.ds(h * half, half)
            piece = rows[pl.ds(n * blocks, blocks), :, at_k].reshape(wide, half)
            term = lax.dot_general(w[at_f, at_k], piece, NT, preferred_element_type=F32)
            prod[n, at_f, :] = term if h == 0 else prod[n, at_f, :] + term
            return carry

        lax.fori_loop(0, 3, matrix, 0)

    def first_half(n, carry):
        multiply(n, 0)
        return carry

    def products(n, carry):
        multiply(n, 1)
        start = pl.multiple_of(n * wide, wide)

        def pointwise(i, carry):
            def rows_of(index):
                return pl.ds(pl.multiple_of(index * hidden + i * tall, tall), tall)

            gate = prod[n, rows_of(0), :]
            up = prod[n, rows_of(1), :]
            back = pltpu.roll(prod[n, rows_of(2), :], wide - CAP, 1)
            sig = jax.nn.sigmoid(gate)
            act = gate * sig
            hid = pltpu.roll(act * up, CAP, 1)
            d_gate = back * up * sig * (1.0 + gate * (1.0 - sig))
            d_up = back * act
            cols = pl.ds(start, wide)
            d_out[rows_of(0), cols] = jnp.where(x_lane, d_gate, 0.0).astype(BF16)
            d_out[rows_of(1), cols] = jnp.where(x_lane, d_up, 0.0).astype(BF16)
            d_out[rows_of(2), cols] = jnp.where(x_lane, 0.0, hid).astype(BF16)
            return carry

        lax.fori_loop(0, hidden // tall, pointwise, 0)
        return carry

    for copy in shares[0]:
        copy.wait_recv()
    lax.fori_loop(0, total // wide, first_half, 0)
    for copy in shares[1]:
        copy.wait_recv()
    lax.fori_loop(0, total // wide, products, 0)

    ordinal = lax.broadcasted_iota(jnp.int32, (n_dp * kept, 1), 0)
    owner = 2 * lax.rem(lax.div(ordinal, kept), chips) + lax.div(ordinal, kept * chips)
    slot = lax.rem(ordinal, kept)
    source = owner * block + lax.div(slot, CAP) * group + lax.rem(slot, CAP)
    select = lax.broadcasted_iota(jnp.int32, (n_dp * kept, total), 1) == source
    d_rows[...] = lax.dot_general(
        jnp.where(select, 1.0, 0.0).astype(BF16), d_out[pl.ds(0, 2 * hidden), :], NT, preferred_element_type=F32
    ).astype(BF16)
    narrow = 256
    chunks = half // narrow
    edges = (0, (chunks + 1) // 2 * narrow, half)

    def lanes_of(h):
        return pl.ds(edges[h], edges[h + 1] - edges[h])

    def terms(i, carry):
        sides = []
        for side in range(2):
            cols = pl.ds(pl.multiple_of(side * half + i * narrow, narrow), narrow)
            term = jnp.dot(d_rows[...], w[pl.ds(0, 2 * hidden), cols], preferred_element_type=F32)
            sides.append(term.reshape(n_dp, kept, narrow))
        both = jnp.concatenate(sides, axis=1).astype(BF16)
        part[:, :, pl.ds(pl.multiple_of(i * narrow, narrow), narrow)] = both
        return carry

    def pair(offset, h):
        k = chip_at(spot + offset)
        return pltpu.make_async_remote_copy(
            src_ref=part.at[(1 - core) * chips + k, :, lanes_of(h)], dst_ref=sib.at[k, :, lanes_of(h)],
            send_sem=pair_send.at[offset, h], recv_sem=pair_recv.at[offset, h],
            device_id=sibling, device_id_type=MESH,
        )

    offsets = [far]
    for step in range(far - 1, 0, -1):
        offsets += [step, chips - step]
    offsets.append(0)
    pairs = {}
    for h in range(2):
        lax.fori_loop(edges[h] // narrow, edges[h + 1] // narrow, terms, 0)
        for offset in offsets:
            pairs[offset, h] = pair(offset, h)
            pairs[offset, h].start()

    def rs(way, step, h):
        return pltpu.make_async_remote_copy(
            src_ref=out_buf.at[way, step, :, lanes_of(h)], dst_ref=in_buf.at[way, step, :, lanes_of(h)],
            send_sem=rs_send.at[way, step, h], recv_sem=rs_recv.at[way, step, h],
            device_id=neighbour[way], device_id_type=MESH,
        )

    def begins(way, step, h):
        return step > 0 or way == h

    strip = 512

    def gradients(first, last):
        def strip_of(i, carry):
            cols = pl.ds(pl.multiple_of(i * strip, strip), strip)
            piece = rows[:, :, cols].reshape(total, strip)

            def matrix(index, carry):
                at_f = pl.ds(pl.multiple_of(index * hidden, hidden), hidden)
                grads_out[at_f, cols] = jnp.dot(d_out[at_f, :], piece, preferred_element_type=F32).astype(BF16)
                return carry

            return lax.fori_loop(0, 3, matrix, carry)

        lax.fori_loop(first, last, strip_of, 0)

    strips = width // strip
    marks = [strips * 2 * step // (2 * far + 1) for step in range(far + 1)]

    ready = set()
    sums = []
    for step in range(far):
        distance = far - step
        for h in range(2):
            cols = lanes_of(h)
            for way in range(2):
                if not begins(way, step, h):
                    continue
                offset = distance if way == 0 else chips - distance
                if (offset, h) not in ready:
                    pairs[offset, h].wait_recv()
                    ready.add((offset, h))
                k = chip_at(spot + offset)
                value = part[core * chips + k, :, cols].astype(F32) + sib[k, :, cols].astype(F32)
                if step > 0 and begins(way, step - 1, h):
                    rs(way, step - 1, h).wait_recv()
                    value += in_buf[way, step - 1, :, cols].astype(F32)
                out_buf[way, step, :, cols] = value.astype(BF16)
                rs(way, step, h).start()
                sums.append((way, step, h))
        gradients(marks[step], marks[step + 1])
    returns = []
    for h in range(2):
        cols = lanes_of(h)
        pairs[0, h].wait_recv()
        own = part[core * chips + chip, :, cols].astype(F32) + sib[chip, :, cols].astype(F32)
        for way in range(2):
            rs(way, far - 1, h).wait_recv()
            own += in_buf[way, far - 1, :, cols].astype(F32)
        returned[mine, :, cols] = own.astype(BF16)
        for step in range(1, window):
            other = lax.rem(mine + step, window)
            returns.append(pltpu.make_async_remote_copy(
                src_ref=returned.at[mine, :, cols], dst_ref=returned.at[mine, :, cols],
                send_sem=z_send.at[step, h], recv_sem=z_recv.at[step, h],
                device_id=(me, other), device_id_type=MESH,
            ))
            returns[-1].start()
    gradients(marks[far], strips)
    for copy in swaps[0] + swaps[1] + hops + shares[0] + shares[1]:
        copy.wait_send()
    for copy in pairs.values():
        copy.wait_send()
    for key in sums:
        rs(*key).wait_send()
    for copy in returns:
        copy.wait()
    back_out[...] = returned[...]


def finish_kernel(hidden, grads, back, pick, token_grad, grad_gate, grad_up, grad_down, summed, sem):
    copies = []
    pieces = sem.shape[1]
    tall = hidden // pieces
    for index, out in enumerate((grad_gate, grad_up, grad_down)):
        for piece in range(pieces):
            copies.append(pltpu.make_async_copy(
                grads.at[pl.ds(index * hidden + piece * tall, tall), :],
                out.at[pl.ds(piece * tall, tall), :], sem.at[index, piece],
            ))
            copies[-1].start()
    window, block, half = back.shape
    returned = back[...].reshape(window * block, half)
    for h in range(2):
        term = jnp.dot(pick[h], returned, preferred_element_type=F32)
        cols = pl.ds(h * half, half)
        summed[:, cols] = term.astype(BF16)
        copies.append(pltpu.make_async_copy(summed.at[:, cols], token_grad.at[:, cols], sem.at[3, h]))
        copies[-1].start()
    for copy in copies:
        copy.wait()


def shards(n_dp, window, tokens, cotangent, experts, route_weight, w_gate, w_up, w_down):
    count, width = tokens.shape
    hidden = w_gate.shape[1]
    half = width // 2
    chips = n_dp // 2
    far = chips // 2
    kept = window * CAP
    block = 2 * kept
    total = n_dp * block
    wide = 256 if total % 256 == 0 else total
    vmem = pl.BlockSpec(memory_space=pltpu.VMEM)
    anywhere = pl.BlockSpec(memory_space=pl.ANY)
    dma = pltpu.SemaphoreType.DMA
    flops = 2 * hidden * width * total
    grads, back, pick = pl.pallas_call(
        functools.partial(exchange_kernel, n_dp, window),
        out_shape=(
            pltpu.VMEM((3 * hidden, width), BF16),
            pltpu.VMEM((window, block, half), BF16),
            pltpu.VMEM((2, count, window * block), BF16),
        ),
        in_specs=[anywhere] * 2 + [vmem] * 2 + [anywhere] * 3,
        out_specs=(vmem, vmem, vmem),
        scratch_shapes=[
            pltpu.VMEM((count, width), BF16),
            pltpu.VMEM((count, width), BF16),
            pltpu.VMEM((window, block, half), BF16),
            pltpu.VMEM((3 * hidden, total), BF16),
            pltpu.VMEM((3 * hidden, width), BF16),
            pltpu.VMEM((window, 4 * CAP, half), BF16),
            pltpu.VMEM((window, 4 * CAP, half), BF16),
            pltpu.VMEM((n_dp, block, width), BF16),
            pltpu.VMEM((total // wide, 3 * hidden, wide), F32),
            pltpu.VMEM((n_dp * kept, 2 * hidden), BF16),
            pltpu.VMEM((n_dp, block, half), BF16),
            pltpu.VMEM((chips, block, half), BF16),
            pltpu.VMEM((2, far, block, half), BF16),
            pltpu.VMEM((2, far, block, half), BF16),
            dma((2, 2)),
            dma((3,)),
            dma((window, 2)),
            dma((window, 2)),
            dma((2, far, 4)),
            dma((2, far, 4)),
            dma((2, far + 1, 4)),
            dma((2, far + 1, 4)),
            dma((chips, 2)),
            dma((chips, 2)),
            dma((2, far, 2)),
            dma((2, far, 2)),
            dma((window, 2)),
            dma((window, 2)),
        ],
        compiler_params=pltpu.CompilerParams(
            collective_id=0, has_side_effects=True, vmem_limit_bytes=61 * 1024 * 1024 - 6 * hidden * width
        ),
        cost_estimate=pl.CostEstimate(
            flops=5 * flops, bytes_accessed=2 * (3 * hidden + 2 * count + total) * width, transcendentals=0
        ),
        name="exchange",
    )(
        tokens, cotangent, experts.T, route_weight.T,
        w_gate[0], w_up[0], w_down[0],
    )

    like = jax.ShapeDtypeStruct((hidden, width), BF16)
    token_grad, grad_g, grad_u, grad_d = pl.pallas_call(
        functools.partial(finish_kernel, hidden),
        out_shape=(jax.ShapeDtypeStruct((count, width), BF16), like, like, like),
        in_specs=[vmem] * 3,
        out_specs=(anywhere,) * 4,
        scratch_shapes=[pltpu.VMEM((count, width), BF16), dma((4, 7 if hidden % 112 == 0 else 2))],
        compiler_params=pltpu.CompilerParams(vmem_limit_bytes=16 * 1024 * 1024),
        cost_estimate=pl.CostEstimate(
            flops=4 * count * window * block * half, bytes_accessed=2 * (3 * hidden + count) * width,
            transcendentals=0,
        ),
        name="finish",
    )(*(pltpu.with_memory_space_constraint(array, pltpu.VMEM) for array in (grads, back, pick)))
    return token_grad, grad_g[None], grad_u[None], grad_d[None]


def solution(mesh):
    by_token = P(("dp", "expert"), None)
    by_expert = P("expert", "dp", None)
    return jax.shard_map(
        functools.partial(shards, mesh.shape["dp"], mesh.shape["expert"]),
        mesh=mesh,
        in_specs=(by_token,) * 4 + (by_expert,) * 3,
        out_specs=(by_token,) + (by_expert,) * 3,
        check_vma=False,
    )
```

```python
import functools

import jax
import jax.numpy as jnp
from jax import lax
from jax.experimental import pallas as pl
from jax.experimental.pallas import tpu as pltpu
from jax.sharding import PartitionSpec as P

CAP = 4
MESH = pl.DeviceIdType.MESH
F32 = jnp.float32
BF16 = jnp.bfloat16
NT = (((1,), (1,)), ((), ()))


def one_hots(experts, place_expert, place_slot):
    count = experts.shape[1]
    first = experts[0:1, :] == place_expert
    second = experts[1:2, :] == place_expert
    named = jnp.where(first | second, 1.0, 0.0).astype(F32)
    shape = (count, count)
    earlier = lax.broadcasted_iota(jnp.int32, shape, 0) < lax.broadcasted_iota(jnp.int32, shape, 1)
    earlier = jnp.where(earlier, 1.0, 0.0).astype(BF16)
    before = jnp.dot(named.astype(BF16), earlier, preferred_element_type=F32)
    return jnp.where(before == place_slot.astype(F32), named, 0.0), first


def exchange_kernel(
    n_dp, window,
    tokens_in, cotangent_in, experts, weights, w_gate, w_up, w_down,
    grads_out, back_out, pick_out,
    tokens, cotangent, returned, d_out, w, sent, arrived, rows, prod, d_rows, part, sib, out_buf, in_buf,
    in_sem, w_sem, y_send, y_recv, ring_send, ring_recv, sib_send, sib_recv,
    pair_send, pair_recv, rs_send, rs_recv, z_send, z_recv,
):
    width = tokens_in.shape[1]
    half = width // 2
    quarter = half // 2
    hidden = w_gate.shape[0]
    chips = n_dp // 2
    far = chips // 2
    group = 2 * CAP
    kept = window * CAP
    block = window * group
    total = n_dp * block

    me = lax.axis_index("dp")
    mine = lax.axis_index("expert")
    core = lax.rem(me, 2)
    chip = lax.div(me, 2)
    spot = jnp.where(lax.rem(chip, 2) == 0, lax.div(chip, 2), chips - 1 - lax.div(chip, 2))

    def chip_at(place):
        place = lax.rem(place + 2 * chips, chips)
        return jnp.where(place < far, 2 * place, 2 * (chips - 1 - place) + 1)

    def at(place):
        return 2 * chip_at(place) + core

    sibling = (2 * chip + 1 - core, mine)
    neighbour = ((at(spot + 1), mine), (at(spot - 1), mine))

    inputs = []
    for p in range(2):
        cols = pl.ds(p * half, half)
        inputs.append([
            pltpu.make_async_copy(tokens_in.at[:, cols], tokens.at[:, cols], in_sem.at[0, p]),
            pltpu.make_async_copy(cotangent_in.at[:, cols], cotangent.at[:, cols], in_sem.at[1, p]),
        ])
        for copy in inputs[-1]:
            copy.start()

    barrier = pltpu.get_barrier_semaphore()
    greet = [sibling, *neighbour]
    for step in range(1, window):
        greet.append((me, lax.rem(mine + step, window)))
    for device in greet:
        pl.semaphore_signal(barrier, inc=1, device_id=device, device_id_type=MESH)

    place = lax.broadcasted_iota(jnp.int32, (block, 1), 0)
    match, first = one_hots(experts[...], lax.div(place, group), lax.rem(place, CAP))
    scale = jnp.where(first, weights[0:1, :], weights[1:2, :]) * match
    scale = jnp.sum(scale, axis=1, keepdims=True)
    is_x = lax.rem(lax.broadcasted_iota(jnp.int32, match.shape, 0), group) < CAP
    x_match = jnp.where(is_x, match, 0.0).astype(BF16)
    c_match = jnp.where(is_x, 0.0, match).astype(BF16)

    def swap(step, p):
        other = lax.rem(mine + step, window)
        lanes = pl.ds(p * quarter, quarter)
        return pltpu.make_async_remote_copy(
            src_ref=sent.at[other, :, lanes], dst_ref=arrived.at[mine, :, lanes],
            send_sem=y_send.at[step, p], recv_sem=y_recv.at[step, p],
            device_id=(me, other), device_id_type=MESH,
        )

    swaps, loads = [], []
    for p in range(2):
        cols = pl.ds(p * half, half)
        for copy in inputs[p]:
            copy.wait()
        slots = jnp.dot(x_match, tokens[:, cols], preferred_element_type=F32)
        slots += scale * jnp.dot(c_match, cotangent[:, cols], preferred_element_type=F32)
        lanes = pl.ds(p * quarter, quarter)
        for e in range(window):
            piece = slots[e * group:(e + 1) * group]
            sent[e, :, lanes] = jnp.concatenate([piece[:, :quarter], piece[:, quarter:]], axis=0).astype(BF16)
        if p == 0:
            pl.semaphore_wait(barrier, len(greet))
        swaps.append([swap(step, p) for step in range(1, window)])
        for copy in swaps[p]:
            copy.start()
        arrived[mine, :, lanes] = sent[mine, :, lanes]
    for index, source in enumerate((w_gate, w_up, w_down)):
        loads.append(pltpu.make_async_copy(source, w.at[pl.ds(index * hidden, hidden), :], w_sem.at[index]))
        loads[-1].start()

    def view(way, step, q):
        origin = at(spot - step) if way == 0 else at(spot + step)
        return rows.at[origin, :, pl.ds(q * quarter, quarter)]

    def hop(way, step, q):
        return pltpu.make_async_remote_copy(
            src_ref=view(way, step, q), dst_ref=view(way, step, q),
            send_sem=ring_send.at[way, step, q], recv_sem=ring_recv.at[way, step, q],
            device_id=neighbour[way], device_id_type=MESH,
        )

    def share(way, step, q):
        return pltpu.make_async_remote_copy(
            src_ref=view(way, step, q), dst_ref=view(way, step, q),
            send_sem=sib_send.at[way, step, q], recv_sem=sib_recv.at[way, step, q],
            device_id=sibling, device_id_type=MESH,
        )

    def travels(way, step, q):
        return step < far - 1 or (step == far - 1 and way == q % 2)

    hops, shares = [], [[], []]
    for p in range(2):
        for copy in swaps[p]:
            copy.wait_recv()
        for q in (2 * p, 2 * p + 1):
            side = (q % 2) * group
            lanes = pl.ds(p * quarter, quarter)
            own = [arrived[s, :, lanes].astype(F32)[side:side + group] for s in range(window)]
            rows[me, :, pl.ds(q * quarter, quarter)] = jnp.concatenate(own, axis=0).astype(BF16)
            for way in range(2):
                if travels(way, 0, q):
                    hops.append(hop(way, 0, q))
                    hops[-1].start()
            shares[p].append(share(0, 0, q))
            shares[p][-1].start()

    columns = window * 2 * kept
    place = lax.broadcasted_iota(jnp.int32, (columns, 1), 0)
    row = lax.rem(place, kept)
    match, _ = one_hots(experts[...], lax.div(place, 2 * kept), lax.rem(row, CAP))
    match = jnp.transpose(jnp.where(lax.div(row, CAP) == mine, match, 0.0))
    side = lax.rem(lax.div(lax.broadcasted_iota(jnp.int32, (1, columns), 1), kept), 2)
    for h in range(2):
        pick_out[h] = jnp.where(side == h, match, 0.0).astype(BF16)

    for step in range(far):
        for q in range(4):
            for way in range(2):
                if travels(way, step, q):
                    hop(way, step, q).wait_recv()
                    if travels(way, step + 1, q):
                        hops.append(hop(way, step + 1, q))
                        hops[-1].start()
                    shares[q // 2].append(share(way, step + 1, q))
                    shares[q // 2][-1].start()
    for copy in loads:
        copy.wait()

    wide = 256 if total % 256 == 0 else total
    blocks = wide // block
    tall = 112 if hidden % 112 == 0 else 16
    x_lane = lax.rem(lax.broadcasted_iota(jnp.int32, (tall, wide), 1), group) < CAP

    def multiply(n, h):
        at_k = pl.ds(h * half, half)
        piece = rows[pl.ds(n * blocks, blocks), :, at_k].reshape(wide, half)
        term = lax.dot_general(w[:, at_k], piece, NT, preferred_element_type=F32)
        prod[n] = term if h == 0 else prod[n] + term

    def first_half(n, carry):
        multiply(n, 0)
        return carry

    def products(n, carry):
        multiply(n, 1)
        start = pl.multiple_of(n * wide, wide)

        def pointwise(i, carry):
            def rows_of(index):
                return pl.ds(pl.multiple_of(index * hidden + i * tall, tall), tall)

            gate = prod[n, rows_of(0), :]
            up = prod[n, rows_of(1), :]
            back = pltpu.roll(prod[n, rows_of(2), :], wide - CAP, 1)
            sig = jax.nn.sigmoid(gate)
            act = gate * sig
            hid = pltpu.roll(act * up, CAP, 1)
            d_gate = back * up * sig * (1.0 + gate * (1.0 - sig))
            d_up = back * act
            cols = pl.ds(start, wide)
            d_out[rows_of(0), cols] = jnp.where(x_lane, d_gate, 0.0).astype(BF16)
            d_out[rows_of(1), cols] = jnp.where(x_lane, d_up, 0.0).astype(BF16)
            d_out[rows_of(2), cols] = jnp.where(x_lane, 0.0, hid).astype(BF16)
            return carry

        lax.fori_loop(0, hidden // tall, pointwise, 0)
        return carry

    for copy in shares[0]:
        copy.wait_recv()
    lax.fori_loop(0, total // wide, first_half, 0)
    for copy in shares[1]:
        copy.wait_recv()
    lax.fori_loop(0, total // wide, products, 0)

    ordinal = lax.broadcasted_iota(jnp.int32, (n_dp * kept, 1), 0)
    owner = 2 * lax.rem(lax.div(ordinal, kept), chips) + lax.div(ordinal, kept * chips)
    slot = lax.rem(ordinal, kept)
    source = owner * block + lax.div(slot, CAP) * group + lax.rem(slot, CAP)
    select = lax.broadcasted_iota(jnp.int32, (n_dp * kept, total), 1) == source
    d_rows[...] = lax.dot_general(
        jnp.where(select, 1.0, 0.0).astype(BF16), d_out[pl.ds(0, 2 * hidden), :], NT, preferred_element_type=F32
    ).astype(BF16)
    narrow = 256
    chunks = half // narrow
    edges = (0, (chunks + 1) // 2 * narrow, half)

    def lanes_of(h):
        return pl.ds(edges[h], edges[h + 1] - edges[h])

    def terms(i, carry):
        sides = []
        for side in range(2):
            cols = pl.ds(pl.multiple_of(side * half + i * narrow, narrow), narrow)
            term = jnp.dot(d_rows[...], w[pl.ds(0, 2 * hidden), cols], preferred_element_type=F32)
            sides.append(term.reshape(n_dp, kept, narrow))
        both = jnp.concatenate(sides, axis=1).astype(BF16)
        part[:, :, pl.ds(pl.multiple_of(i * narrow, narrow), narrow)] = both
        return carry

    def pair(offset, h):
        k = chip_at(spot + offset)
        return pltpu.make_async_remote_copy(
            src_ref=part.at[(1 - core) * chips + k, :, lanes_of(h)], dst_ref=sib.at[k, :, lanes_of(h)],
            send_sem=pair_send.at[offset, h], recv_sem=pair_recv.at[offset, h],
            device_id=sibling, device_id_type=MESH,
        )

    offsets = [far]
    for step in range(far - 1, 0, -1):
        offsets += [step, chips - step]
    offsets.append(0)
    pairs = {}
    for h in range(2):
        lax.fori_loop(edges[h] // narrow, edges[h + 1] // narrow, terms, 0)
        for offset in offsets:
            pairs[offset, h] = pair(offset, h)
            pairs[offset, h].start()

    def rs(way, step, h):
        return pltpu.make_async_remote_copy(
            src_ref=out_buf.at[way, step, :, lanes_of(h)], dst_ref=in_buf.at[way, step, :, lanes_of(h)],
            send_sem=rs_send.at[way, step, h], recv_sem=rs_recv.at[way, step, h],
            device_id=neighbour[way], device_id_type=MESH,
        )

    def begins(way, step, h):
        return step > 0 or way == h

    strip = 256
    strips = width // strip
    gaps = 2 * far + 3
    done = 0

    def strip_of(i, carry):
        cols = pl.ds(pl.multiple_of(i * strip, strip), strip)
        piece = rows[:, :, cols].reshape(total, strip)
        grads_out[:, cols] = jnp.dot(d_out[...], piece, preferred_element_type=F32).astype(BF16)
        return carry

    def gradients(first, gap):
        last = strips if gap == gaps else strips * gap // gaps
        lax.fori_loop(first, last, strip_of, 0)
        return last

    ready = set()
    sums = []
    for step in range(far):
        distance = far - step
        for h in range(2):
            cols = lanes_of(h)
            for way in range(2):
                if not begins(way, step, h):
                    continue
                offset = distance if way == 0 else chips - distance
                if (offset, h) not in ready:
                    pairs[offset, h].wait_recv()
                    ready.add((offset, h))
                k = chip_at(spot + offset)
                value = part[core * chips + k, :, cols].astype(F32) + sib[k, :, cols].astype(F32)
                if step > 0 and begins(way, step - 1, h):
                    rs(way, step - 1, h).wait_recv()
                    value += in_buf[way, step - 1, :, cols].astype(F32)
                out_buf[way, step, :, cols] = value.astype(BF16)
                rs(way, step, h).start()
                sums.append((way, step, h))
            done = gradients(done, 2 * step + h + 1)
    returns = []
    for h in range(2):
        cols = lanes_of(h)
        pairs[0, h].wait_recv()
        own = part[core * chips + chip, :, cols].astype(F32) + sib[chip, :, cols].astype(F32)
        for way in range(2):
            rs(way, far - 1, h).wait_recv()
            own += in_buf[way, far - 1, :, cols].astype(F32)
        returned[mine, :, cols] = own.astype(BF16)
        for step in range(1, window):
            other = lax.rem(mine + step, window)
            returns.append(pltpu.make_async_remote_copy(
                src_ref=returned.at[mine, :, cols], dst_ref=returned.at[mine, :, cols],
                send_sem=z_send.at[step, h], recv_sem=z_recv.at[step, h],
                device_id=(me, other), device_id_type=MESH,
            ))
            returns[-1].start()
    gradients(done, gaps)
    for copy in swaps[0] + swaps[1] + hops + shares[0] + shares[1]:
        copy.wait_send()
    for copy in pairs.values():
        copy.wait_send()
    for key in sums:
        rs(*key).wait_send()
    for copy in returns:
        copy.wait()
    back_out[...] = returned[...]


def finish_kernel(hidden, grads, back, pick, token_grad, grad_gate, grad_up, grad_down, summed, sem):
    copies = []
    pieces = sem.shape[1]
    tall = hidden // pieces
    for index, out in enumerate((grad_gate, grad_up, grad_down)):
        for piece in range(pieces):
            copies.append(pltpu.make_async_copy(
                grads.at[pl.ds(index * hidden + piece * tall, tall), :],
                out.at[pl.ds(piece * tall, tall), :], sem.at[index, piece],
            ))
            copies[-1].start()
    window, block, half = back.shape
    returned = back[...].reshape(window * block, half)
    for h in range(2):
        term = jnp.dot(pick[h], returned, preferred_element_type=F32)
        cols = pl.ds(h * half, half)
        summed[:, cols] = term.astype(BF16)
        copies.append(pltpu.make_async_copy(summed.at[:, cols], token_grad.at[:, cols], sem.at[3, h]))
        copies[-1].start()
    for copy in copies:
        copy.wait()


def shards(n_dp, window, tokens, cotangent, experts, route_weight, w_gate, w_up, w_down):
    count, width = tokens.shape
    hidden = w_gate.shape[1]
    half = width // 2
    chips = n_dp // 2
    far = chips // 2
    kept = window * CAP
    block = 2 * kept
    total = n_dp * block
    wide = 256 if total % 256 == 0 else total
    vmem = pl.BlockSpec(memory_space=pltpu.VMEM)
    anywhere = pl.BlockSpec(memory_space=pl.ANY)
    dma = pltpu.SemaphoreType.DMA
    flops = 2 * hidden * width * total
    grads, back, pick = pl.pallas_call(
        functools.partial(exchange_kernel, n_dp, window),
        out_shape=(
            pltpu.VMEM((3 * hidden, width), BF16),
            pltpu.VMEM((window, block, half), BF16),
            pltpu.VMEM((2, count, window * block), BF16),
        ),
        in_specs=[anywhere] * 2 + [vmem] * 2 + [anywhere] * 3,
        out_specs=(vmem, vmem, vmem),
        scratch_shapes=[
            pltpu.VMEM((count, width), BF16),
            pltpu.VMEM((count, width), BF16),
            pltpu.VMEM((window, block, half), BF16),
            pltpu.VMEM((3 * hidden, total), BF16),
            pltpu.VMEM((3 * hidden, width), BF16),
            pltpu.VMEM((window, 4 * CAP, half), BF16),
            pltpu.VMEM((window, 4 * CAP, half), BF16),
            pltpu.VMEM((n_dp, block, width), BF16),
            pltpu.VMEM((total // wide, 3 * hidden, wide), F32),
            pltpu.VMEM((n_dp * kept, 2 * hidden), BF16),
            pltpu.VMEM((n_dp, block, half), BF16),
            pltpu.VMEM((chips, block, half), BF16),
            pltpu.VMEM((2, far, block, half), BF16),
            pltpu.VMEM((2, far, block, half), BF16),
            dma((2, 2)),
            dma((3,)),
            dma((window, 2)),
            dma((window, 2)),
            dma((2, far, 4)),
            dma((2, far, 4)),
            dma((2, far + 1, 4)),
            dma((2, far + 1, 4)),
            dma((chips, 2)),
            dma((chips, 2)),
            dma((2, far, 2)),
            dma((2, far, 2)),
            dma((window, 2)),
            dma((window, 2)),
        ],
        compiler_params=pltpu.CompilerParams(
            collective_id=0, has_side_effects=True, vmem_limit_bytes=61 * 1024 * 1024 - 6 * hidden * width
        ),
        cost_estimate=pl.CostEstimate(
            flops=5 * flops, bytes_accessed=2 * (3 * hidden + 2 * count + total) * width, transcendentals=0
        ),
        name="exchange",
    )(
        tokens, cotangent, experts.T, route_weight.T,
        w_gate[0], w_up[0], w_down[0],
    )

    like = jax.ShapeDtypeStruct((hidden, width), BF16)
    token_grad, grad_g, grad_u, grad_d = pl.pallas_call(
        functools.partial(finish_kernel, hidden),
        out_shape=(jax.ShapeDtypeStruct((count, width), BF16), like, like, like),
        in_specs=[vmem] * 3,
        out_specs=(anywhere,) * 4,
        scratch_shapes=[pltpu.VMEM((count, width), BF16), dma((4, 7 if hidden % 112 == 0 else 2))],
        compiler_params=pltpu.CompilerParams(vmem_limit_bytes=16 * 1024 * 1024),
        cost_estimate=pl.CostEstimate(
            flops=4 * count * window * block * half, bytes_accessed=2 * (3 * hidden + count) * width,
            transcendentals=0,
        ),
        name="finish",
    )(*(pltpu.with_memory_space_constraint(array, pltpu.VMEM) for array in (grads, back, pick)))
    return token_grad, grad_g[None], grad_u[None], grad_d[None]


def solution(mesh):
    by_token = P(("dp", "expert"), None)
    by_expert = P("expert", "dp", None)
    return jax.shard_map(
        functools.partial(shards, mesh.shape["dp"], mesh.shape["expert"]),
        mesh=mesh,
        in_specs=(by_token,) * 4 + (by_expert,) * 3,
        out_specs=(by_token,) + (by_expert,) * 3,
        check_vma=False,
    )
```

```python
import functools

import jax
import jax.numpy as jnp
from jax import lax
from jax.experimental import pallas as pl
from jax.experimental.pallas import tpu as pltpu
from jax.sharding import PartitionSpec as P

CAP = 4
MESH = pl.DeviceIdType.MESH
F32 = jnp.float32
BF16 = jnp.bfloat16
NT = (((1,), (1,)), ((), ()))


def one_hots(experts, place_expert, place_slot):
    count = experts.shape[1]
    first = experts[0:1, :] == place_expert
    second = experts[1:2, :] == place_expert
    named = jnp.where(first | second, 1.0, 0.0).astype(F32)
    shape = (count, count)
    earlier = lax.broadcasted_iota(jnp.int32, shape, 0) < lax.broadcasted_iota(jnp.int32, shape, 1)
    earlier = jnp.where(earlier, 1.0, 0.0).astype(BF16)
    before = jnp.dot(named.astype(BF16), earlier, preferred_element_type=F32)
    return jnp.where(before == place_slot.astype(F32), named, 0.0), first


def exchange_kernel(
    n_dp, window,
    tokens_in, cotangent_in, experts, weights, w_gate, w_up, w_down,
    grads_out, back_out, pick_out,
    tokens, cotangent, returned, d_out, w, sent, arrived, rows, prod, d_rows, part, sib, out_buf, in_buf,
    in_sem, w_sem, y_send, y_recv, ring_send, ring_recv, sib_send, sib_recv,
    pair_send, pair_recv, rs_send, rs_recv, z_send, z_recv,
):
    width = tokens_in.shape[1]
    half = width // 2
    quarter = half // 2
    hidden = w_gate.shape[0]
    chips = n_dp // 2
    far = chips // 2
    group = 2 * CAP
    kept = window * CAP
    block = window * group
    total = n_dp * block

    me = lax.axis_index("dp")
    mine = lax.axis_index("expert")
    core = lax.rem(me, 2)
    chip = lax.div(me, 2)
    spot = jnp.where(lax.rem(chip, 2) == 0, lax.div(chip, 2), chips - 1 - lax.div(chip, 2))

    def chip_at(place):
        place = lax.rem(place + 2 * chips, chips)
        return jnp.where(place < far, 2 * place, 2 * (chips - 1 - place) + 1)

    def at(place):
        return 2 * chip_at(place) + core

    sibling = (2 * chip + 1 - core, mine)
    neighbour = ((at(spot + 1), mine), (at(spot - 1), mine))

    inputs = []
    for p in range(2):
        cols = pl.ds(p * half, half)
        inputs.append([
            pltpu.make_async_copy(tokens_in.at[:, cols], tokens.at[:, cols], in_sem.at[0, p]),
            pltpu.make_async_copy(cotangent_in.at[:, cols], cotangent.at[:, cols], in_sem.at[1, p]),
        ])
        for copy in inputs[-1]:
            copy.start()

    barrier = pltpu.get_barrier_semaphore()
    greet = [sibling, *neighbour]
    for step in range(1, window):
        greet.append((me, lax.rem(mine + step, window)))
    for device in greet:
        pl.semaphore_signal(barrier, inc=1, device_id=device, device_id_type=MESH)

    place = lax.broadcasted_iota(jnp.int32, (block, 1), 0)
    match, first = one_hots(experts[...], lax.div(place, group), lax.rem(place, CAP))
    scale = jnp.where(first, weights[0:1, :], weights[1:2, :]) * match
    scale = jnp.sum(scale, axis=1, keepdims=True)
    is_x = lax.rem(lax.broadcasted_iota(jnp.int32, match.shape, 0), group) < CAP
    x_match = jnp.where(is_x, match, 0.0).astype(BF16)
    c_match = jnp.where(is_x, 0.0, match).astype(BF16)

    def swap(step, p):
        other = lax.rem(mine + step, window)
        lanes = pl.ds(p * quarter, quarter)
        return pltpu.make_async_remote_copy(
            src_ref=sent.at[other, :, lanes], dst_ref=arrived.at[mine, :, lanes],
            send_sem=y_send.at[step, p], recv_sem=y_recv.at[step, p],
            device_id=(me, other), device_id_type=MESH,
        )

    swaps, loads = [], []
    for p in range(2):
        cols = pl.ds(p * half, half)
        for copy in inputs[p]:
            copy.wait()
        slots = jnp.dot(x_match, tokens[:, cols], preferred_element_type=F32)
        slots += scale * jnp.dot(c_match, cotangent[:, cols], preferred_element_type=F32)
        lanes = pl.ds(p * quarter, quarter)
        for e in range(window):
            piece = slots[e * group:(e + 1) * group]
            sent[e, :, lanes] = jnp.concatenate([piece[:, :quarter], piece[:, quarter:]], axis=0).astype(BF16)
        if p == 0:
            pl.semaphore_wait(barrier, len(greet))
        swaps.append([swap(step, p) for step in range(1, window)])
        for copy in swaps[p]:
            copy.start()
        arrived[mine, :, lanes] = sent[mine, :, lanes]
    for index, source in enumerate((w_gate, w_up, w_down)):
        loads.append(pltpu.make_async_copy(source, w.at[pl.ds(index * hidden, hidden), :], w_sem.at[index]))
        loads[-1].start()

    def view(way, step, q):
        origin = at(spot - step) if way == 0 else at(spot + step)
        return rows.at[origin, :, pl.ds(q * quarter, quarter)]

    def hop(way, step, q):
        return pltpu.make_async_remote_copy(
            src_ref=view(way, step, q), dst_ref=view(way, step, q),
            send_sem=ring_send.at[0], recv_sem=ring_recv.at[way, step, q],
            device_id=neighbour[way], device_id_type=MESH,
        )

    def share(way, step, q):
        return pltpu.make_async_remote_copy(
            src_ref=view(way, step, q), dst_ref=view(way, step, q),
            send_sem=sib_send.at[q // 2], recv_sem=sib_recv.at[q // 2],
            device_id=sibling, device_id_type=MESH,
        )

    def all_hops():
        every = rows.at[pl.ds(0, chips - 1)]
        return pltpu.make_async_remote_copy(
            src_ref=every, dst_ref=every, send_sem=ring_send.at[0], recv_sem=sib_recv.at[0],
            device_id=sibling, device_id_type=MESH,
        )

    def all_shares(p):
        every = rows.at[pl.ds(0, chips), :, pl.ds(p * half, half)]
        return pltpu.make_async_remote_copy(
            src_ref=every, dst_ref=every, send_sem=sib_send.at[p], recv_sem=sib_recv.at[p],
            device_id=sibling, device_id_type=MESH,
        )

    def travels(way, step, q):
        return step < far - 1 or (step == far - 1 and way == q % 2)

    for p in range(2):
        for copy in swaps[p]:
            copy.wait_recv()
        for q in (2 * p, 2 * p + 1):
            side = (q % 2) * group
            lanes = pl.ds(p * quarter, quarter)
            own = [arrived[s, :, lanes].astype(F32)[side:side + group] for s in range(window)]
            rows[me, :, pl.ds(q * quarter, quarter)] = jnp.concatenate(own, axis=0).astype(BF16)
            for way in range(2):
                if travels(way, 0, q):
                    hop(way, 0, q).start()
            share(0, 0, q).start()

    columns = window * 2 * kept
    place = lax.broadcasted_iota(jnp.int32, (columns, 1), 0)
    row = lax.rem(place, kept)
    match, _ = one_hots(experts[...], lax.div(place, 2 * kept), lax.rem(row, CAP))
    match = jnp.transpose(jnp.where(lax.div(row, CAP) == mine, match, 0.0))
    side = lax.rem(lax.div(lax.broadcasted_iota(jnp.int32, (1, columns), 1), kept), 2)
    for h in range(2):
        pick_out[h] = jnp.where(side == h, match, 0.0).astype(BF16)

    for step in range(far):
        for q in range(4):
            for way in range(2):
                if travels(way, step, q):
                    hop(way, step, q).wait_recv()
                    if travels(way, step + 1, q):
                        hop(way, step + 1, q).start()
                    share(way, step + 1, q).start()
    for copy in loads:
        copy.wait()

    wide = 256 if total % 256 == 0 else total
    blocks = wide // block
    tall = 112 if hidden % 112 == 0 else 16
    x_lane = lax.rem(lax.broadcasted_iota(jnp.int32, (tall, wide), 1), group) < CAP

    def multiply(n, h):
        def matrix(index, carry):
            at_f = pl.ds(pl.multiple_of(index * hidden, hidden), hidden)
            at_k = pl.ds(h * half, half)
            piece = rows[pl.ds(n * blocks, blocks), :, at_k].reshape(wide, half)
            term = lax.dot_general(w[at_f, at_k], piece, NT, preferred_element_type=F32)
            prod[n, at_f, :] = term if h == 0 else prod[n, at_f, :] + term
            return carry

        lax.fori_loop(0, 3, matrix, 0)

    def first_half(n, carry):
        multiply(n, 0)
        return carry

    def products(n, carry):
        multiply(n, 1)
        start = pl.multiple_of(n * wide, wide)

        def pointwise(i, carry):
            def rows_of(index):
                return pl.ds(pl.multiple_of(index * hidden + i * tall, tall), tall)

            gate = prod[n, rows_of(0), :]
            up = prod[n, rows_of(1), :]
            back = pltpu.roll(prod[n, rows_of(2), :], wide - CAP, 1)
            sig = jax.nn.sigmoid(gate)
            act = gate * sig
            hid = pltpu.roll(act * up, CAP, 1)
            d_gate = back * up * sig * (1.0 + gate * (1.0 - sig))
            d_up = back * act
            cols = pl.ds(start, wide)
            d_out[rows_of(0), cols] = jnp.where(x_lane, d_gate, 0.0).astype(BF16)
            d_out[rows_of(1), cols] = jnp.where(x_lane, d_up, 0.0).astype(BF16)
            d_out[rows_of(2), cols] = jnp.where(x_lane, 0.0, hid).astype(BF16)
            return carry

        lax.fori_loop(0, hidden // tall, pointwise, 0)
        return carry

    all_shares(0).wait_recv()
    lax.fori_loop(0, total // wide, first_half, 0)
    all_shares(1).wait_recv()
    lax.fori_loop(0, total // wide, products, 0)

    ordinal = lax.broadcasted_iota(jnp.int32, (n_dp * kept, 1), 0)
    owner = 2 * lax.rem(lax.div(ordinal, kept), chips) + lax.div(ordinal, kept * chips)
    slot = lax.rem(ordinal, kept)
    source = owner * block + lax.div(slot, CAP) * group + lax.rem(slot, CAP)
    select = lax.broadcasted_iota(jnp.int32, (n_dp * kept, total), 1) == source
    d_rows[...] = lax.dot_general(
        jnp.where(select, 1.0, 0.0).astype(BF16), d_out[pl.ds(0, 2 * hidden), :], NT, preferred_element_type=F32
    ).astype(BF16)
    narrow = 256
    chunks = half // narrow
    edges = (0, (chunks + 1) // 2 * narrow, half)

    def lanes_of(h):
        return pl.ds(edges[h], edges[h + 1] - edges[h])

    def terms(i, carry):
        sides = []
        for side in range(2):
            cols = pl.ds(pl.multiple_of(side * half + i * narrow, narrow), narrow)
            term = jnp.dot(d_rows[...], w[pl.ds(0, 2 * hidden), cols], preferred_element_type=F32)
            sides.append(term.reshape(n_dp, kept, narrow))
        both = jnp.concatenate(sides, axis=1).astype(BF16)
        part[:, :, pl.ds(pl.multiple_of(i * narrow, narrow), narrow)] = both
        return carry

    def pair(offset, h):
        k = chip_at(spot + offset)
        return pltpu.make_async_remote_copy(
            src_ref=part.at[(1 - core) * chips + k, :, lanes_of(h)], dst_ref=sib.at[k, :, lanes_of(h)],
            send_sem=pair_send.at[0], recv_sem=pair_recv.at[offset, h],
            device_id=sibling, device_id_type=MESH,
        )

    offsets = [far]
    for step in range(far - 1, 0, -1):
        offsets += [step, chips - step]
    offsets.append(0)
    pairs = {}
    for h in range(2):
        lax.fori_loop(edges[h] // narrow, edges[h + 1] // narrow, terms, 0)
        for offset in offsets:
            pairs[offset, h] = pair(offset, h)
            pairs[offset, h].start()

    def rs(way, step, h):
        return pltpu.make_async_remote_copy(
            src_ref=out_buf.at[way, step, :, lanes_of(h)], dst_ref=in_buf.at[way, step, :, lanes_of(h)],
            send_sem=rs_send.at[way, step, h], recv_sem=rs_recv.at[way, step, h],
            device_id=neighbour[way], device_id_type=MESH,
        )

    def begins(way, step, h):
        return step > 0 or way == h

    strip = 512

    def gradients(first, last):
        def strip_of(i, carry):
            cols = pl.ds(pl.multiple_of(i * strip, strip), strip)
            piece = rows[:, :, cols].reshape(total, strip)

            def matrix(index, carry):
                at_f = pl.ds(pl.multiple_of(index * hidden, hidden), hidden)
                grads_out[at_f, cols] = jnp.dot(d_out[at_f, :], piece, preferred_element_type=F32).astype(BF16)
                return carry

            return lax.fori_loop(0, 3, matrix, carry)

        lax.fori_loop(first, last, strip_of, 0)

    strips = width // strip
    marks = [strips * 2 * step // (2 * far + 1) for step in range(far + 1)]

    ready = set()
    sums = []
    for step in range(far):
        distance = far - step
        for h in range(2):
            cols = lanes_of(h)
            for way in range(2):
                if not begins(way, step, h):
                    continue
                offset = distance if way == 0 else chips - distance
                if (offset, h) not in ready:
                    pairs[offset, h].wait_recv()
                    ready.add((offset, h))
                k = chip_at(spot + offset)
                value = part[core * chips + k, :, cols].astype(F32) + sib[k, :, cols].astype(F32)
                if step > 0 and begins(way, step - 1, h):
                    rs(way, step - 1, h).wait_recv()
                    value += in_buf[way, step - 1, :, cols].astype(F32)
                out_buf[way, step, :, cols] = value.astype(BF16)
                rs(way, step, h).start()
                sums.append((way, step, h))
        gradients(marks[step], marks[step + 1])
    returns = []
    for h in range(2):
        cols = lanes_of(h)
        pairs[0, h].wait_recv()
        own = part[core * chips + chip, :, cols].astype(F32) + sib[chip, :, cols].astype(F32)
        for way in range(2):
            rs(way, far - 1, h).wait_recv()
            own += in_buf[way, far - 1, :, cols].astype(F32)
        returned[mine, :, cols] = own.astype(BF16)
        for step in range(1, window):
            other = lax.rem(mine + step, window)
            returns.append(pltpu.make_async_remote_copy(
                src_ref=returned.at[mine, :, cols], dst_ref=returned.at[mine, :, cols],
                send_sem=z_send.at[step, h], recv_sem=z_recv.at[step, h],
                device_id=(me, other), device_id_type=MESH,
            ))
            returns[-1].start()
    gradients(marks[far], strips)
    for copy in swaps[0] + swaps[1]:
        copy.wait_send()
    all_hops().wait_send()
    for p in range(2):
        all_shares(p).wait_send()
    pltpu.make_async_remote_copy(
        src_ref=part.at[pl.ds(0, chips)], dst_ref=sib, send_sem=pair_send.at[0], recv_sem=pair_recv.at[0, 0],
        device_id=sibling, device_id_type=MESH,
    ).wait_send()
    for key in sums:
        rs(*key).wait_send()
    for copy in returns:
        copy.wait()
    back_out[...] = returned[...]


def finish_kernel(hidden, grads, back, pick, token_grad, grad_gate, grad_up, grad_down, summed, sem):
    copies = []
    pieces = sem.shape[1]
    tall = hidden // pieces
    for index, out in enumerate((grad_gate, grad_up, grad_down)):
        for piece in range(pieces):
            copies.append(pltpu.make_async_copy(
                grads.at[pl.ds(index * hidden + piece * tall, tall), :],
                out.at[pl.ds(piece * tall, tall), :], sem.at[index, piece],
            ))
            copies[-1].start()
    window, block, half = back.shape
    returned = back[...].reshape(window * block, half)
    for h in range(2):
        term = jnp.dot(pick[h], returned, preferred_element_type=F32)
        cols = pl.ds(h * half, half)
        summed[:, cols] = term.astype(BF16)
        copies.append(pltpu.make_async_copy(summed.at[:, cols], token_grad.at[:, cols], sem.at[3, h]))
        copies[-1].start()
    for copy in copies:
        copy.wait()


def shards(n_dp, window, tokens, cotangent, experts, route_weight, w_gate, w_up, w_down):
    count, width = tokens.shape
    hidden = w_gate.shape[1]
    half = width // 2
    chips = n_dp // 2
    far = chips // 2
    kept = window * CAP
    block = 2 * kept
    total = n_dp * block
    wide = 256 if total % 256 == 0 else total
    vmem = pl.BlockSpec(memory_space=pltpu.VMEM)
    anywhere = pl.BlockSpec(memory_space=pl.ANY)
    dma = pltpu.SemaphoreType.DMA
    flops = 2 * hidden * width * total
    grads, back, pick = pl.pallas_call(
        functools.partial(exchange_kernel, n_dp, window),
        out_shape=(
            pltpu.VMEM((3 * hidden, width), BF16),
            pltpu.VMEM((window, block, half), BF16),
            pltpu.VMEM((2, count, window * block), BF16),
        ),
        in_specs=[anywhere] * 2 + [vmem] * 2 + [anywhere] * 3,
        out_specs=(vmem, vmem, vmem),
        scratch_shapes=[
            pltpu.VMEM((count, width), BF16),
            pltpu.VMEM((count, width), BF16),
            pltpu.VMEM((window, block, half), BF16),
            pltpu.VMEM((3 * hidden, total), BF16),
            pltpu.VMEM((3 * hidden, width), BF16),
            pltpu.VMEM((window, 4 * CAP, half), BF16),
            pltpu.VMEM((window, 4 * CAP, half), BF16),
            pltpu.VMEM((n_dp, block, width), BF16),
            pltpu.VMEM((total // wide, 3 * hidden, wide), F32),
            pltpu.VMEM((n_dp * kept, 2 * hidden), BF16),
            pltpu.VMEM((n_dp, block, half), BF16),
            pltpu.VMEM((chips, block, half), BF16),
            pltpu.VMEM((2, far, block, half), BF16),
            pltpu.VMEM((2, far, block, half), BF16),
            dma((2, 2)),
            dma((3,)),
            dma((window, 2)),
            dma((window, 2)),
            dma((1,)),
            dma((2, far, 4)),
            dma((2,)),
            dma((2,)),
            dma((1,)),
            dma((chips, 2)),
            dma((2, far, 2)),
            dma((2, far, 2)),
            dma((window, 2)),
            dma((window, 2)),
        ],
        compiler_params=pltpu.CompilerParams(
            collective_id=0, has_side_effects=True, vmem_limit_bytes=61 * 1024 * 1024 - 6 * hidden * width
        ),
        cost_estimate=pl.CostEstimate(
            flops=5 * flops, bytes_accessed=2 * (3 * hidden + 2 * count + total) * width, transcendentals=0
        ),
        name="exchange",
    )(
        tokens, cotangent, experts.T, route_weight.T,
        w_gate[0], w_up[0], w_down[0],
    )

    like = jax.ShapeDtypeStruct((hidden, width), BF16)
    token_grad, grad_g, grad_u, grad_d = pl.pallas_call(
        functools.partial(finish_kernel, hidden),
        out_shape=(jax.ShapeDtypeStruct((count, width), BF16), like, like, like),
        in_specs=[vmem] * 3,
        out_specs=(anywhere,) * 4,
        scratch_shapes=[pltpu.VMEM((count, width), BF16), dma((4, 7 if hidden % 112 == 0 else 2))],
        compiler_params=pltpu.CompilerParams(vmem_limit_bytes=16 * 1024 * 1024),
        cost_estimate=pl.CostEstimate(
            flops=4 * count * window * block * half, bytes_accessed=2 * (3 * hidden + count) * width,
            transcendentals=0,
        ),
        name="finish",
    )(*(pltpu.with_memory_space_constraint(array, pltpu.VMEM) for array in (grads, back, pick)))
    return token_grad, grad_g[None], grad_u[None], grad_d[None]


def solution(mesh):
    by_token = P(("dp", "expert"), None)
    by_expert = P("expert", "dp", None)
    return jax.shard_map(
        functools.partial(shards, mesh.shape["dp"], mesh.shape["expert"]),
        mesh=mesh,
        in_specs=(by_token,) * 4 + (by_expert,) * 3,
        out_specs=(by_token,) + (by_expert,) * 3,
        check_vma=False,
    )
```

```python
import functools

import jax
import jax.numpy as jnp
from jax import lax
from jax.experimental import pallas as pl
from jax.experimental.pallas import tpu as pltpu
from jax.sharding import PartitionSpec as P

CAP = 4
MESH = pl.DeviceIdType.MESH
F32 = jnp.float32
BF16 = jnp.bfloat16
NT = (((1,), (1,)), ((), ()))


def one_hots(experts, place_expert, place_slot):
    count = experts.shape[1]
    first = experts[0:1, :] == place_expert
    second = experts[1:2, :] == place_expert
    named = jnp.where(first | second, 1.0, 0.0).astype(F32)
    shape = (count, count)
    earlier = lax.broadcasted_iota(jnp.int32, shape, 0) < lax.broadcasted_iota(jnp.int32, shape, 1)
    earlier = jnp.where(earlier, 1.0, 0.0).astype(BF16)
    before = jnp.dot(named.astype(BF16), earlier, preferred_element_type=F32)
    return jnp.where(before == place_slot.astype(F32), named, 0.0), first


def exchange_kernel(
    n_dp, window,
    tokens_in, cotangent_in, experts, weights, w_gate, w_up, w_down,
    grads_out, back_out, pick_out,
    select, tokens, cotangent, returned, d_out, w, sent, arrived, rows, prod, d_rows, part, sib, out_buf, in_buf,
    in_sem, w_sem, y_send, y_recv, ring_send, ring_recv, sib_send, sib_recv,
    pair_send, pair_recv, rs_send, rs_recv, z_send, z_recv,
):
    width = tokens_in.shape[1]
    half = width // 2
    quarter = half // 2
    hidden = w_gate.shape[0]
    chips = n_dp // 2
    far = chips // 2
    group = 2 * CAP
    kept = window * CAP
    block = window * group
    total = n_dp * block

    me = lax.axis_index("dp")
    mine = lax.axis_index("expert")
    core = lax.rem(me, 2)
    chip = lax.div(me, 2)
    spot = jnp.where(lax.rem(chip, 2) == 0, lax.div(chip, 2), chips - 1 - lax.div(chip, 2))

    ring = []
    for offset in range(chips):
        place = spot + offset
        place = jnp.where(place >= chips, place - chips, place)
        ring.append(jnp.where(place < far, 2 * place, 2 * (chips - 1 - place) + 1))

    def at(offset):
        return 2 * ring[offset % chips] + core

    sibling = (2 * chip + 1 - core, mine)
    neighbour = ((at(1), mine), (at(-1), mine))

    inputs = []
    for p in range(2):
        cols = pl.ds(p * half, half)
        inputs.append([
            pltpu.make_async_copy(tokens_in.at[:, cols], tokens.at[:, cols], in_sem.at[0, p]),
            pltpu.make_async_copy(cotangent_in.at[:, cols], cotangent.at[:, cols], in_sem.at[1, p]),
        ])
        for copy in inputs[-1]:
            copy.start()

    barrier = pltpu.get_barrier_semaphore()
    greet = [sibling, *neighbour]
    for step in range(1, window):
        greet.append((me, lax.rem(mine + step, window)))
    for device in greet:
        pl.semaphore_signal(barrier, inc=1, device_id=device, device_id_type=MESH)

    place = lax.broadcasted_iota(jnp.int32, (block, 1), 0)
    match, first = one_hots(experts[...], lax.div(place, group), lax.rem(place, CAP))
    scale = jnp.where(first, weights[0:1, :], weights[1:2, :]) * match
    scale = jnp.sum(scale, axis=1, keepdims=True)
    is_x = lax.rem(lax.broadcasted_iota(jnp.int32, match.shape, 0), group) < CAP
    x_match = jnp.where(is_x, match, 0.0).astype(BF16)
    c_match = jnp.where(is_x, 0.0, match).astype(BF16)

    def swap(step, p):
        other = lax.rem(mine + step, window)
        lanes = pl.ds(p * quarter, quarter)
        return pltpu.make_async_remote_copy(
            src_ref=sent.at[other, :, lanes], dst_ref=arrived.at[mine, :, lanes],
            send_sem=y_send.at[step, p], recv_sem=y_recv.at[step, p],
            device_id=(me, other), device_id_type=MESH,
        )

    swaps, loads = [], []
    for p in range(2):
        cols = pl.ds(p * half, half)
        for copy in inputs[p]:
            copy.wait()
        slots = jnp.dot(x_match, tokens[:, cols], preferred_element_type=F32)
        slots += scale * jnp.dot(c_match, cotangent[:, cols], preferred_element_type=F32)
        lanes = pl.ds(p * quarter, quarter)
        for e in range(window):
            piece = slots[e * group:(e + 1) * group]
            sent[e, :, lanes] = jnp.concatenate([piece[:, :quarter], piece[:, quarter:]], axis=0).astype(BF16)
        if p == 0:
            pl.semaphore_wait(barrier, len(greet))
        swaps.append([swap(step, p) for step in range(1, window)])
        for copy in swaps[p]:
            copy.start()
        arrived[mine, :, lanes] = sent[mine, :, lanes]
    for index, source in enumerate((w_gate, w_up, w_down)):
        loads.append(pltpu.make_async_copy(source, w.at[pl.ds(index * hidden, hidden), :], w_sem.at[index]))
        loads[-1].start()

    def view(way, step, q):
        origin = at(-step) if way == 0 else at(step)
        return rows.at[origin, :, pl.ds(q * quarter, quarter)]

    def hop(way, step, q):
        piece = view(way, step, q)
        return pltpu.make_async_remote_copy(
            src_ref=piece, dst_ref=piece,
            send_sem=ring_send.at[0], recv_sem=ring_recv.at[way, step, q],
            device_id=neighbour[way], device_id_type=MESH,
        )

    def share(way, step, q):
        piece = view(way, step, q)
        return pltpu.make_async_remote_copy(
            src_ref=piece, dst_ref=piece,
            send_sem=sib_send.at[q // 2], recv_sem=sib_recv.at[q // 2],
            device_id=sibling, device_id_type=MESH,
        )

    def all_hops():
        every = rows.at[pl.ds(0, chips - 1)]
        return pltpu.make_async_remote_copy(
            src_ref=every, dst_ref=every, send_sem=ring_send.at[0], recv_sem=sib_recv.at[0],
            device_id=sibling, device_id_type=MESH,
        )

    def all_shares(p):
        every = rows.at[pl.ds(0, chips), :, pl.ds(p * half, half)]
        return pltpu.make_async_remote_copy(
            src_ref=every, dst_ref=every, send_sem=sib_send.at[p], recv_sem=sib_recv.at[p],
            device_id=sibling, device_id_type=MESH,
        )

    def travels(way, step, q):
        return step < far - 1 or (step == far - 1 and way == q % 2)

    for p in range(2):
        for copy in swaps[p]:
            copy.wait_recv()
        for q in (2 * p, 2 * p + 1):
            side = (q % 2) * group
            lanes = pl.ds(p * quarter, quarter)
            own = [arrived[s, :, lanes].astype(F32)[side:side + group] for s in range(window)]
            rows[me, :, pl.ds(q * quarter, quarter)] = jnp.concatenate(own, axis=0).astype(BF16)
            for way in range(2):
                if travels(way, 0, q):
                    hop(way, 0, q).start()
            share(0, 0, q).start()

    columns = window * 2 * kept
    place = lax.broadcasted_iota(jnp.int32, (columns, 1), 0)
    row = lax.rem(place, kept)
    match, _ = one_hots(experts[...], lax.div(place, 2 * kept), lax.rem(row, CAP))
    match = jnp.transpose(jnp.where(lax.div(row, CAP) == mine, match, 0.0))
    side = lax.rem(lax.div(lax.broadcasted_iota(jnp.int32, (1, columns), 1), kept), 2)
    for h in range(2):
        pick_out[h] = jnp.where(side == h, match, 0.0).astype(BF16)

    ordinal = lax.broadcasted_iota(jnp.int32, (n_dp * kept, 1), 0)
    owner = 2 * lax.rem(lax.div(ordinal, kept), chips) + lax.div(ordinal, kept * chips)
    slot = lax.rem(ordinal, kept)
    select[...] = owner * block + lax.div(slot, CAP) * group + lax.rem(slot, CAP)

    for step in range(far):
        for q in range(4):
            for way in range(2):
                if travels(way, step, q):
                    hop(way, step, q).wait_recv()
                    if travels(way, step + 1, q):
                        hop(way, step + 1, q).start()
                    share(way, step + 1, q).start()
    for copy in loads:
        copy.wait()

    wide = 256 if total % 256 == 0 else total
    blocks = wide // block
    tall = 112 if hidden % 112 == 0 else 16
    x_lane = (lax.broadcasted_iota(jnp.int32, (tall, wide), 1) & (group - 1)) < CAP

    def multiply(n, h):
        def matrix(index, carry):
            at_f = pl.ds(pl.multiple_of(index * hidden, hidden), hidden)
            at_k = pl.ds(h * half, half)
            piece = rows[pl.ds(n * blocks, blocks), :, at_k].reshape(wide, half)
            term = lax.dot_general(w[at_f, at_k], piece, NT, preferred_element_type=F32)
            prod[n, at_f, :] = term if h == 0 else prod[n, at_f, :] + term
            return carry

        lax.fori_loop(0, 3, matrix, 0)

    def first_half(n, carry):
        multiply(n, 0)
        return carry

    def products(n, carry):
        multiply(n, 1)
        start = pl.multiple_of(n * wide, wide)

        def pointwise(i, carry):
            def rows_of(index):
                return pl.ds(pl.multiple_of(index * hidden + i * tall, tall), tall)

            gate = prod[n, rows_of(0), :]
            up = prod[n, rows_of(1), :]
            back = pltpu.roll(prod[n, rows_of(2), :], wide - CAP, 1)
            sig = jax.nn.sigmoid(gate)
            act = gate * sig
            hid = pltpu.roll(act * up, CAP, 1)
            d_gate = back * up * sig * (1.0 + gate * (1.0 - sig))
            d_up = back * act
            cols = pl.ds(start, wide)
            d_out[rows_of(0), cols] = jnp.where(x_lane, d_gate, 0.0).astype(BF16)
            d_out[rows_of(1), cols] = jnp.where(x_lane, d_up, 0.0).astype(BF16)
            d_out[rows_of(2), cols] = jnp.where(x_lane, 0.0, hid).astype(BF16)
            return carry

        lax.fori_loop(0, hidden // tall, pointwise, 0)
        return carry

    all_shares(0).wait_recv()
    lax.fori_loop(0, total // wide, first_half, 0)
    all_shares(1).wait_recv()
    lax.fori_loop(0, total // wide, products, 0)

    chosen = lax.broadcasted_iota(jnp.int32, (n_dp * kept, total), 1) == select[...]
    d_rows[...] = lax.dot_general(
        jnp.where(chosen, 1.0, 0.0).astype(BF16), d_out[pl.ds(0, 2 * hidden), :], NT, preferred_element_type=F32
    ).astype(BF16)
    narrow = 256
    chunks = half // narrow
    edges = (0, (chunks + 1) // 2 * narrow, half)

    def lanes_of(h):
        return pl.ds(edges[h], edges[h + 1] - edges[h])

    def terms(i, carry):
        sides = []
        for side in range(2):
            cols = pl.ds(pl.multiple_of(side * half + i * narrow, narrow), narrow)
            term = jnp.dot(d_rows[...], w[pl.ds(0, 2 * hidden), cols], preferred_element_type=F32)
            sides.append(term.reshape(n_dp, kept, narrow))
        both = jnp.concatenate(sides, axis=1).astype(BF16)
        part[:, :, pl.ds(pl.multiple_of(i * narrow, narrow), narrow)] = both
        return carry

    def pair(offset, h):
        k = ring[offset]
        return pltpu.make_async_remote_copy(
            src_ref=part.at[(1 - core) * chips + k, :, lanes_of(h)], dst_ref=sib.at[k, :, lanes_of(h)],
            send_sem=pair_send.at[0], recv_sem=pair_recv.at[offset, h],
            device_id=sibling, device_id_type=MESH,
        )

    offsets = [far]
    for step in range(far - 1, 0, -1):
        offsets += [step, chips - step]
    offsets.append(0)
    pairs = {}
    for h in range(2):
        lax.fori_loop(edges[h] // narrow, edges[h + 1] // narrow, terms, 0)
        for offset in offsets:
            pairs[offset, h] = pair(offset, h)
            pairs[offset, h].start()

    def rs(way, step, h):
        return pltpu.make_async_remote_copy(
            src_ref=out_buf.at[way, step, :, lanes_of(h)], dst_ref=in_buf.at[way, step, :, lanes_of(h)],
            send_sem=rs_send.at[way, step, h], recv_sem=rs_recv.at[way, step, h],
            device_id=neighbour[way], device_id_type=MESH,
        )

    def begins(way, step, h):
        return step > 0 or way == h

    strip = 512

    def gradients(first, last):
        def strip_of(i, carry):
            cols = pl.ds(pl.multiple_of(i * strip, strip), strip)
            piece = rows[:, :, cols].reshape(total, strip)

            def matrix(index, carry):
                at_f = pl.ds(pl.multiple_of(index * hidden, hidden), hidden)
                grads_out[at_f, cols] = jnp.dot(d_out[at_f, :], piece, preferred_element_type=F32).astype(BF16)
                return carry

            return lax.fori_loop(0, 3, matrix, carry)

        lax.fori_loop(first, last, strip_of, 0)

    strips = width // strip
    marks = [strips * 2 * step // (2 * far + 1) for step in range(far + 1)]

    ready = set()
    sums = []
    for step in range(far):
        distance = far - step
        for h in range(2):
            cols = lanes_of(h)
            for way in range(2):
                if not begins(way, step, h):
                    continue
                offset = distance if way == 0 else chips - distance
                if (offset, h) not in ready:
                    pairs[offset, h].wait_recv()
                    ready.add((offset, h))
                k = ring[offset]
                value = part[core * chips + k, :, cols].astype(F32) + sib[k, :, cols].astype(F32)
                if step > 0 and begins(way, step - 1, h):
                    rs(way, step - 1, h).wait_recv()
                    value += in_buf[way, step - 1, :, cols].astype(F32)
                out_buf[way, step, :, cols] = value.astype(BF16)
                rs(way, step, h).start()
                sums.append((way, step, h))
        gradients(marks[step], marks[step + 1])
    returns = []
    for h in range(2):
        cols = lanes_of(h)
        pairs[0, h].wait_recv()
        own = part[core * chips + chip, :, cols].astype(F32) + sib[chip, :, cols].astype(F32)
        for way in range(2):
            rs(way, far - 1, h).wait_recv()
            own += in_buf[way, far - 1, :, cols].astype(F32)
        returned[mine, :, cols] = own.astype(BF16)
        for step in range(1, window):
            other = lax.rem(mine + step, window)
            returns.append(pltpu.make_async_remote_copy(
                src_ref=returned.at[mine, :, cols], dst_ref=returned.at[mine, :, cols],
                send_sem=z_send.at[step, h], recv_sem=z_recv.at[step, h],
                device_id=(me, other), device_id_type=MESH,
            ))
            returns[-1].start()
    gradients(marks[far], strips)
    for copy in swaps[0] + swaps[1]:
        copy.wait_send()
    all_hops().wait_send()
    for p in range(2):
        all_shares(p).wait_send()
    pltpu.make_async_remote_copy(
        src_ref=part.at[pl.ds(0, chips)], dst_ref=sib, send_sem=pair_send.at[0], recv_sem=pair_recv.at[0, 0],
        device_id=sibling, device_id_type=MESH,
    ).wait_send()
    for key in sums:
        rs(*key).wait_send()
    for copy in returns:
        copy.wait()
    back_out[...] = returned[...]


def finish_kernel(hidden, grads, back, pick, token_grad, grad_gate, grad_up, grad_down, summed, sem):
    copies = []
    pieces = sem.shape[1]
    tall = hidden // pieces
    for index, out in enumerate((grad_gate, grad_up, grad_down)):
        for piece in range(pieces):
            copies.append(pltpu.make_async_copy(
                grads.at[pl.ds(index * hidden + piece * tall, tall), :],
                out.at[pl.ds(piece * tall, tall), :], sem.at[index, piece],
            ))
            copies[-1].start()
    window, block, half = back.shape
    returned = back[...].reshape(window * block, half)
    for h in range(2):
        term = jnp.dot(pick[h], returned, preferred_element_type=F32)
        cols = pl.ds(h * half, half)
        summed[:, cols] = term.astype(BF16)
        copies.append(pltpu.make_async_copy(summed.at[:, cols], token_grad.at[:, cols], sem.at[3, h]))
        copies[-1].start()
    for copy in copies:
        copy.wait()


def shards(n_dp, window, tokens, cotangent, experts, route_weight, w_gate, w_up, w_down):
    count, width = tokens.shape
    hidden = w_gate.shape[1]
    half = width // 2
    chips = n_dp // 2
    far = chips // 2
    kept = window * CAP
    block = 2 * kept
    total = n_dp * block
    wide = 256 if total % 256 == 0 else total
    vmem = pl.BlockSpec(memory_space=pltpu.VMEM)
    anywhere = pl.BlockSpec(memory_space=pl.ANY)
    dma = pltpu.SemaphoreType.DMA
    flops = 2 * hidden * width * total
    grads, back, pick = pl.pallas_call(
        functools.partial(exchange_kernel, n_dp, window),
        out_shape=(
            pltpu.VMEM((3 * hidden, width), BF16),
            pltpu.VMEM((window, block, half), BF16),
            pltpu.VMEM((2, count, window * block), BF16),
        ),
        in_specs=[anywhere] * 2 + [vmem] * 2 + [anywhere] * 3,
        out_specs=(vmem, vmem, vmem),
        scratch_shapes=[
            pltpu.VMEM((n_dp * kept, 1), jnp.int32),
            pltpu.VMEM((count, width), BF16),
            pltpu.VMEM((count, width), BF16),
            pltpu.VMEM((window, block, half), BF16),
            pltpu.VMEM((3 * hidden, total), BF16),
            pltpu.VMEM((3 * hidden, width), BF16),
            pltpu.VMEM((window, 4 * CAP, half), BF16),
            pltpu.VMEM((window, 4 * CAP, half), BF16),
            pltpu.VMEM((n_dp, block, width), BF16),
            pltpu.VMEM((total // wide, 3 * hidden, wide), F32),
            pltpu.VMEM((n_dp * kept, 2 * hidden), BF16),
            pltpu.VMEM((n_dp, block, half), BF16),
            pltpu.VMEM((chips, block, half), BF16),
            pltpu.VMEM((2, far, block, half), BF16),
            pltpu.VMEM((2, far, block, half), BF16),
            dma((2, 2)),
            dma((3,)),
            dma((window, 2)),
            dma((window, 2)),
            dma((1,)),
            dma((2, far, 4)),
            dma((2,)),
            dma((2,)),
            dma((1,)),
            dma((chips, 2)),
            dma((2, far, 2)),
            dma((2, far, 2)),
            dma((window, 2)),
            dma((window, 2)),
        ],
        compiler_params=pltpu.CompilerParams(
            collective_id=0, has_side_effects=True, vmem_limit_bytes=61 * 1024 * 1024 - 6 * hidden * width
        ),
        cost_estimate=pl.CostEstimate(
            flops=5 * flops, bytes_accessed=2 * (3 * hidden + 2 * count + total) * width, transcendentals=0
        ),
        name="exchange",
    )(
        tokens, cotangent, experts.T, route_weight.T,
        w_gate[0], w_up[0], w_down[0],
    )

    like = jax.ShapeDtypeStruct((hidden, width), BF16)
    token_grad, grad_g, grad_u, grad_d = pl.pallas_call(
        functools.partial(finish_kernel, hidden),
        out_shape=(jax.ShapeDtypeStruct((count, width), BF16), like, like, like),
        in_specs=[vmem] * 3,
        out_specs=(anywhere,) * 4,
        scratch_shapes=[pltpu.VMEM((count, width), BF16), dma((4, 7 if hidden % 112 == 0 else 2))],
        compiler_params=pltpu.CompilerParams(vmem_limit_bytes=16 * 1024 * 1024),
        cost_estimate=pl.CostEstimate(
            flops=4 * count * window * block * half, bytes_accessed=2 * (3 * hidden + count) * width,
            transcendentals=0,
        ),
        name="finish",
    )(*(pltpu.with_memory_space_constraint(array, pltpu.VMEM) for array in (grads, back, pick)))
    return token_grad, grad_g[None], grad_u[None], grad_d[None]


def solution(mesh):
    by_token = P(("dp", "expert"), None)
    by_expert = P("expert", "dp", None)
    return jax.shard_map(
        functools.partial(shards, mesh.shape["dp"], mesh.shape["expert"]),
        mesh=mesh,
        in_specs=(by_token,) * 4 + (by_expert,) * 3,
        out_specs=(by_token,) + (by_expert,) * 3,
        check_vma=False,
    )
```
